32 devices in a mesh: groups: 2 (over y), row: 8 (over z, x), col: 2 (over core).
Axes of the slice: x: 2, y: 2, z: 4, core: 2. Of those that a mesh axis runs over, the one named last changes fastest.
Arguments:
- tile_blocks: bfloat16 [256, 128, 128], P(('groups', 'row', 'col')), parts along dimension 0, may hold values from -0.25 to 0.25
- tile_rows: int32 [256], P(('groups', 'row', 'col')), parts along dimension 0, may hold values from 0 to 127, as said below
- tile_cols: int32 [256], P(('groups', 'row', 'col')), parts along dimension 0, may hold values from 0 to 31, as said below
- saved_primal: bfloat16 [4, 64, 32, 128], P(None, ('groups', 'row')), parts along dimension 1, may hold values from -6 to 6
- saved_dual: bfloat16 [3, 256, 32, 128], P(None, ('groups', 'row', 'col')), parts along dimension 1, may hold values from -6 to 6
- primal_active: int32 [3, 64, 128], P(None, ('groups', 'row')), parts along dimension 1, may hold values 0 or 1
- dual_active: int32 [3, 256, 128], P(None, ('groups', 'row', 'col')), parts along dimension 1, may hold values 0 or 1
- primal_mix: float32 [3, 32, 32], replicated, may hold values from -1 to 1
- dual_mix: float32 [3, 32, 32], replicated, may hold values from -1 to 1
- step_fracs: int32 [3, 4], replicated, may hold values from 2 to 9, as said below
- cot_primal: float32 [64, 32, 128], P(('groups', 'row')), parts along dimension 0, may hold values from -6 to 6
- cot_dual: float32 [256, 32, 128], P(('groups', 'row', 'col')), parts along dimension 0, may hold values from -6 to 6
Outputs:
- grad_primal: float32 [64, 32, 128], P(('groups', 'row')), parts along dimension 0
- grad_dual: float32 [256, 32, 128], P(('groups', 'row', 'col')), parts along dimension 0
- grad_primal_mix: float32 [6, 32, 32], P('groups'), parts along dimension 0
- grad_dual_mix: float32 [6, 32, 32], P('groups'), parts along dimension 0
The draws below stay inside these ranges and needn't reach their ends.
There are 2 independent parts, one for each index of `groups`. The reference program is written for one: setup_inputs(seed, part) draws one part's arguments, and reference() takes and returns one part's arrays. A program takes and returns all parts, laid end to end along the dimension named above; an argument that names none is the same for every part. Nothing has to cross between parts.
Inputs may be any that keep to these rules, and one draw needn't show every extreme that they name: `tile_rows`: tiles come in blocks of 8, one block per device in the order of row then col. Dual block b belongs to the device numbered b // 8 in that order. The tiles of the device with row index r and col index c lie in primal blocks r * 4 to (r + 1) * 4 - 1 and in dual blocks of devices with col index c, exactly one tile in the dual blocks of the devices of each row index. `tile_cols`: see tile_rows. `step_fracs`: numerators lie in 2 to 4, denominators in 6 to 9.
All inputs are finite; a program needn't handle non-finite values. No bound on the sum of `primal_active` or of `dual_active` on one device may be relied on, other than what follows from the above.
Results may differ from the reference program's by a relative error of at most 0.007.
Values may be sent and summed in bfloat16 or wider, within the bound.
No kernel may reach another device: no remote copies, remote signals or barrier semaphores. Data moves between devices by JAX's collectives and lax.ppermute only.
A program may use at most 64 MiB of HBM per device.

```python
import math
import jax
import jax.numpy as jnp
from jax import lax

C = 32
TB = 128
LAYERS = 3
PRIMAL_BLOCKS = 4
DUAL_OWN = 8
TILE_DEV = 8
TILES = 128
CBLK = 32
RBLK = 128
N_ROW = 8
N_COL = 2


def peer_order(key):
    return jax.random.permutation(key, N_ROW).astype(jnp.int32)


def tile_layout(key):
    device_count = N_ROW * N_COL
    peer_key, dual_key, primal_key = jax.random.split(key, 3)
    orders = jax.vmap(peer_order)(jax.random.split(peer_key, device_count))
    orders = orders.at[0].set((orders[0] - orders[0, 0]) % N_ROW)
    last_order = orders[device_count - 1]
    orders = orders.at[device_count - 1].set((last_order + N_ROW - 1 - last_order[0]) % N_ROW)
    local_dual = jax.random.randint(dual_key, (device_count, TILE_DEV), 0, DUAL_OWN, dtype=jnp.int32)
    local_dual = local_dual.at[0, 0].set(0).at[device_count - 1, 0].set(DUAL_OWN - 1)
    local_primal = jax.random.randint(primal_key, (device_count, TILE_DEV), 0, PRIMAL_BLOCKS, dtype=jnp.int32)
    local_primal = local_primal.at[0, 0].set(0).at[device_count - 1, 0].set(PRIMAL_BLOCKS - 1)
    devices = jnp.arange(device_count, dtype=jnp.int32)
    row_index = devices // N_COL
    col_index = devices % N_COL
    rows = (orders * N_COL + col_index[:, None]) * DUAL_OWN + local_dual
    cols = row_index[:, None] * PRIMAL_BLOCKS + local_primal
    return (rows.reshape(-1).astype(jnp.int32), cols.reshape(-1).astype(jnp.int32))


def draw_tile_rows(key, part):
    return tile_layout(key)[0]


def draw_tile_cols(key, part):
    return tile_layout(key)[1]


def draw_step_fracs(key, part):
    key = jax.random.fold_in(key, 7)
    upper_key, lower_key = jax.random.split(key)
    numerators = jax.random.randint(upper_key, (LAYERS, 2), 2, 5, dtype=jnp.int32)
    denominators = jax.random.randint(lower_key, (LAYERS, 2), 6, 10, dtype=jnp.int32)
    return jnp.stack([numerators[:, 0], denominators[:, 0], numerators[:, 1], denominators[:, 1]], axis=1)


def with_ends(entries, own_key, smallest, largest):
    longest = entries.shape.index(max(entries.shape))
    spots = []
    for shift in (0, 1):
        where = [jax.random.randint(jax.random.fold_in(own_key, axis), (), 0, length) for axis, length in enumerate(entries.shape)]
        where[longest] = (where[longest] + shift) % entries.shape[longest]
        spots.append(tuple(where))
    return entries.at[spots[0]].set(smallest).at[spots[1]].set(largest)


def block_levels(rng, extent, cuts, low, top_value):
    factor_of, own = 1.0, jax.random.fold_in(rng, 6)
    for dim, shards_of in cuts:
        steps = jnp.exp(jax.random.uniform(jax.random.fold_in(own, dim), (shards_of,), jnp.float32, low / len(cuts), top_value / len(cuts)))
        factor_of = factor_of * jnp.repeat(steps, extent[dim] // shards_of).reshape([-1 if axis == dim else 1 for axis in range(len(extent))])
    return factor_of


def bell_draw(own_key, dims, scale, reach, cuts=(), kind=jnp.bfloat16):
    level = block_levels(own_key, dims, cuts, -0.22, 0.18) if cuts else 1.0
    drawn = jax.random.normal(own_key, dims, jnp.float32) * scale * level
    return jnp.minimum(jnp.maximum(drawn, -reach), reach).astype(kind)


def setup_inputs(seed: int = 0, part: int = 0) -> dict:
    key_list = jax.random.split(jax.random.key(seed), 13)
    part_keys = jax.random.split(jax.random.fold_in(key_list[12], part), 13)
    tile_blocks = bell_draw(part_keys[0], (TILES, TB, TB), (TB * N_ROW * N_COL // PRIMAL_BLOCKS) ** -0.5, 0.25, ((0, 16),))
    tile_rows = draw_tile_rows(jax.random.fold_in(jax.random.fold_in(key_list[12], part), 71), part)
    tile_cols = draw_tile_cols(jax.random.fold_in(jax.random.fold_in(key_list[12], part), 71), part)
    saved_primal = bell_draw(part_keys[3], (LAYERS + 1, CBLK, C, TB), 1.0, 6.0, ((1, 8),))
    saved_dual = bell_draw(part_keys[4], (LAYERS, RBLK, C, TB), 1.0, 6.0, ((1, 16),))
    primal_active = with_ends((jax.random.randint(part_keys[5], (LAYERS, CBLK, TB), 0, 4) < 3).astype(jnp.int32), jax.random.fold_in(part_keys[5], 1), 0, 1)
    dual_active = with_ends((jax.random.randint(part_keys[6], (LAYERS, RBLK, TB), 0, 4) < 3).astype(jnp.int32), jax.random.fold_in(part_keys[6], 1), 0, 1)
    primal_mix = bell_draw(key_list[7], (LAYERS, C, C), C ** -0.5, 1.0, (), jnp.float32)
    dual_mix = bell_draw(key_list[8], (LAYERS, C, C), C ** -0.5, 1.0, (), jnp.float32)
    step_fracs = draw_step_fracs(jax.random.fold_in(key_list[12], 71), part)
    cot_primal = bell_draw(part_keys[10], (CBLK, C, TB), 1.0, 6.0, ((0, 8),), jnp.float32)
    cot_dual = bell_draw(part_keys[11], (RBLK, C, TB), 1.0, 6.0, ((0, 16),), jnp.float32)
    return dict(tile_blocks=tile_blocks, tile_rows=tile_rows, tile_cols=tile_cols, saved_primal=saved_primal, saved_dual=saved_dual, primal_active=primal_active, dual_active=dual_active, primal_mix=primal_mix, dual_mix=dual_mix, step_fracs=step_fracs, cot_primal=cot_primal, cot_dual=cot_dual)


def forward_all(tile_blocks, tile_rows, tile_cols, primal, segments):
    tiles_grouped = tile_blocks.reshape(-1, TILE_DEV, TB, TB)
    rows_grouped = tile_rows.reshape(-1, TILE_DEV)
    cols_grouped = tile_cols.reshape(-1, TILE_DEV)

    def accumulate(total, pieces):
        block_tiles, row_ids, col_ids = pieces
        picked = jnp.take(primal, col_ids, axis=0).astype(jnp.float32)
        product = jnp.einsum('tij,tcj->tci', block_tiles.astype(jnp.float32), picked, precision=lax.Precision.HIGHEST)
        rounded = lax.optimization_barrier(product.astype(jnp.bfloat16)).astype(jnp.float32)
        return (total + jax.ops.segment_sum(rounded, row_ids, num_segments=segments), None)
    start = jnp.zeros((segments, primal.shape[1], TB), jnp.float32)
    return lax.scan(accumulate, start, (tiles_grouped, rows_grouped, cols_grouped))[0]

def adjoint_all(tile_blocks, tile_rows, tile_cols, dual_part, segments):
    tiles_grouped = tile_blocks.reshape(-1, TILE_DEV, TB, TB)
    rows_grouped = tile_rows.reshape(-1, TILE_DEV)
    cols_grouped = tile_cols.reshape(-1, TILE_DEV)

    def accumulate(total, pieces):
        block_tiles, row_ids, col_ids = pieces
        picked = jnp.take(dual_part, row_ids, axis=0).astype(jnp.float32)
        product = jnp.einsum('tij,tci->tcj', block_tiles.astype(jnp.float32), picked, precision=lax.Precision.HIGHEST)
        return (total + jax.ops.segment_sum(product, col_ids, num_segments=segments), None)
    start = jnp.zeros((segments, dual_part.shape[1], TB), jnp.float32)
    return lax.scan(accumulate, start, (tiles_grouped, rows_grouped, cols_grouped))[0]

def reference(tile_blocks, tile_rows, tile_cols, saved_primal, saved_dual, primal_active, dual_active, primal_mix, dual_mix, step_fracs, cot_primal, cot_dual):
    highest = lax.Precision.HIGHEST
    fractions = step_fracs.astype(jnp.float32)
    primal_steps = fractions[:, 0] / fractions[:, 1]
    dual_steps = fractions[:, 2] / fractions[:, 3]
    row_scale = 1.0 / math.sqrt(RBLK * TB)
    col_scale = 1.0 / math.sqrt(CBLK * TB)
    grad_x = cot_primal
    grad_y = cot_dual
    primal_terms = [None] * LAYERS
    dual_terms = [None] * LAYERS
    for layer_id in reversed(range(LAYERS)):
        tau_now = primal_steps[layer_id]
        sigma_now = dual_steps[layer_id]
        dual_cot = dual_active[layer_id][:, None, :].astype(jnp.float32) * grad_y
        mixed_dual = (-sigma_now * jnp.einsum('ce,bei->bci', dual_mix[layer_id], dual_cot, precision=highest)).astype(jnp.bfloat16)
        back_primal = adjoint_all(tile_blocks, tile_rows, tile_cols, mixed_dual, CBLK)
        primal_cot = primal_active[layer_id][:, None, :].astype(jnp.float32) * (grad_x + 2.0 * back_primal)
        mixed_primal = (-tau_now * jnp.einsum('ce,bei->bci', primal_mix[layer_id], primal_cot, precision=highest)).astype(jnp.bfloat16)
        extrapolated = (2.0 * saved_primal[layer_id + 1].astype(jnp.float32) - saved_primal[layer_id].astype(jnp.float32)).astype(jnp.bfloat16)
        images = forward_all(tile_blocks, tile_rows, tile_cols, extrapolated, RBLK)
        pulled = adjoint_all(tile_blocks, tile_rows, tile_cols, saved_dual[layer_id], CBLK)
        dual_terms[layer_id] = -sigma_now * row_scale * jnp.einsum('bci,bei->ce', images, dual_cot, precision=highest)
        primal_terms[layer_id] = -tau_now * col_scale * jnp.einsum('bci,bei->ce', pulled, primal_cot, precision=highest)
        grad_x = primal_cot - back_primal
        grad_y = dual_cot + forward_all(tile_blocks, tile_rows, tile_cols, mixed_primal, RBLK)
    return (grad_x, grad_y, jnp.stack(primal_terms), jnp.stack(dual_terms))
```

```python
from functools import partial
import math

import jax
import jax.numpy as jnp
from jax import lax
from jax.experimental import pallas as pl
from jax.experimental.pallas import tpu as pltpu
from jax.sharding import PartitionSpec as P

SMEM = pl.BlockSpec(memory_space=pltpu.SMEM)
VMEM = pl.BlockSpec(memory_space=pltpu.VMEM)
F32 = jnp.float32
BF16 = jnp.bfloat16
PARAMS = pltpu.CompilerParams(vmem_limit_bytes=16 * 1024 * 1024)


def loop(count, body):
    if count <= 16:
        for i in range(count):
            body(i)
    else:
        lax.fori_loop(0, count, lambda i, _: (body(i), 0)[1], 0)


def exact_dot(a, b, dims):
    return lax.dot_general(
        a, b, (dims, ((), ())), precision=lax.Precision.HIGHEST, preferred_element_type=F32
    )


def mask_and_send(layer, mask_ref, saved_ref, index_ref, cot_ref, send_ref):
    owned, channels, _ = cot_ref.shape
    for b in range(owned):
        cot_ref[b] = mask_ref[layer, pl.ds(b, 1), :].astype(F32) * cot_ref[b]

    def one(r):
        d = index_ref[0, r]
        send_ref[r, :channels, :] = cot_ref[d].astype(BF16)
        send_ref[r, channels:, :] = saved_ref[layer, d]

    loop(send_ref.shape[0], one)


def add_pushed(index_ref, received_ref, cot_ref):
    channels = cot_ref.shape[1]

    def one(r):
        d = index_ref[0, r]
        cot_ref[d] = cot_ref[d] + received_ref[r, :channels, :].astype(F32)

    loop(received_ref.shape[0], one)


def sum_terms(received_ref):
    channels = received_ref.shape[1] // 2
    rows = received_ref.shape[0]
    if rows <= 16:
        total = received_ref[0, channels:, :].astype(F32)
        for r in range(1, rows):
            total = total + received_ref[r, channels:, :].astype(F32)
    else:
        total = lax.fori_loop(
            0,
            rows,
            lambda r, t: t + received_ref[r, channels:, :].astype(F32),
            jnp.zeros((channels, received_ref.shape[2]), F32),
        )
    return total + pltpu.roll(total, total.shape[1] // 2, 1)


def first_dual_kernel(layer, index_ref, cot_in, mask_ref, saved_ref, cot_ref, send_ref):
    cot_ref[...] = cot_in[...]
    mask_and_send(layer, mask_ref, saved_ref, index_ref, cot_ref, send_ref)


def dual_kernel(
    layer, index_ref, received_ref, cot_in, mask_ref, saved_ref, cot_ref, send_ref, terms_ref
):
    cot_ref[...] = cot_in[...]
    add_pushed(index_ref, received_ref, cot_ref)
    mask_and_send(layer, mask_ref, saved_ref, index_ref, cot_ref, send_ref)
    terms_ref[...] = sum_terms(received_ref)


def last_dual_kernel(index_ref, received_ref, cot_in, cot_ref, terms_ref):
    cot_ref[...] = cot_in[...]
    add_pushed(index_ref, received_ref, cot_ref)
    terms_ref[...] = sum_terms(received_ref)


def pull_kernel(index_ref, tiles_ref, received_ref, sum_ref):
    sum_ref[...] = jnp.zeros_like(sum_ref)

    def one(t):
        product = jnp.dot(received_ref[index_ref[1, t]], tiles_ref[t], preferred_element_type=F32)
        p = index_ref[2, t]
        sum_ref[p] = sum_ref[p] + product

    loop(tiles_ref.shape[0], one)


def primal_kernel(
    layer,
    index_ref,
    steps_ref,
    tiles_ref,
    mine_ref,
    other_ref,
    grad_in,
    mask_ref,
    saved_ref,
    dual_mix_ref,
    primal_mix_ref,
    grad_ref,
    send_ref,
    mixed_ref,
):
    blocks, channels, side = grad_ref.shape
    sigma = steps_ref[layer, 1]
    tau = steps_ref[layer, 0]
    pad = jnp.zeros((side - 2 * channels, side), F32)
    none = jnp.zeros((channels, side), F32)
    terms = jnp.zeros((channels, side), F32)
    for p in range(blocks):
        both = mine_ref[p] + other_ref[p]
        pulled_mixed, pulled_saved = both[:channels], both[channels:]
        back = -sigma * exact_dot(dual_mix_ref[layer], pulled_mixed, ((1,), (0,)))
        primal_cot = mask_ref[layer, pl.ds(p, 1), :].astype(F32) * (grad_in[p] + 2.0 * back)
        grad_ref[p] = primal_cot - back
        mixed_ref[p] = (
            -tau * exact_dot(primal_mix_ref[layer], primal_cot, ((1,), (0,)))
        ).astype(BF16)
        extrapolated = (
            2.0 * saved_ref[layer + 1, p].astype(F32) - saved_ref[layer, p].astype(F32)
        ).astype(BF16).astype(F32)
        terms = terms + exact_dot(
            extrapolated, jnp.concatenate([pulled_mixed, none, pad], 0), ((1,), (1,))
        )
        terms = terms + exact_dot(
            pulled_saved, jnp.concatenate([none, primal_cot, pad], 0), ((1,), (1,))
        )
    high = terms.astype(BF16).astype(F32)
    packed = (high + pltpu.roll(terms - high, side // 2, 1)).astype(BF16)

    def one(t):
        product = lax.dot_general(
            mixed_ref[index_ref[2, t]],
            tiles_ref[t],
            (((1,), (1,)), ((), ())),
            preferred_element_type=F32,
        )
        peer = index_ref[1, t]
        send_ref[peer, :channels, :] = product.astype(BF16)
        send_ref[peer, channels:, :] = packed

    loop(tiles_ref.shape[0], one)


def per_device(
    tile_blocks,
    tile_rows,
    tile_cols,
    saved_primal,
    saved_dual,
    primal_active,
    dual_active,
    primal_mix,
    dual_mix,
    step_fracs,
    cot_primal,
    cot_dual,
):
    row_count = lax.axis_size("row")
    col_count = lax.axis_size("col")
    owned, channels, side = cot_dual.shape
    primal_count = cot_primal.shape[0]
    layer_count = primal_mix.shape[0]
    row_scale = 1.0 / math.sqrt(owned * row_count * col_count * side)
    col_scale = 1.0 / math.sqrt(primal_count * row_count * side)
    local_cols = tile_cols % primal_count
    peers = tile_rows // (owned * col_count)
    peer_ids = jnp.arange(row_count, dtype=jnp.int32)
    wanted = jnp.sum(
        jnp.where(peers[None, :] == peer_ids[:, None], (tile_rows % owned)[None, :], 0), axis=1
    )

    def exchange(x):
        return lax.all_to_all(x, "row", split_axis=0, concat_axis=0, tiled=True)

    incoming = exchange(wanted)
    index = jnp.stack([incoming, peers, local_cols])
    fractions = step_fracs.astype(F32)
    steps = jnp.stack(
        [fractions[:, 0] / fractions[:, 1], fractions[:, 2] / fractions[:, 3]], axis=1
    )
    swap = [(i, col_count - 1 - i) for i in range(col_count)]
    message = jax.ShapeDtypeStruct((row_count, 2 * channels, side), BF16)
    dual_shape = jax.ShapeDtypeStruct(cot_dual.shape, F32)
    terms_shape = jax.ShapeDtypeStruct((channels, side), F32)
    grad_x, cot = cot_primal, cot_dual
    received = None
    all_terms = []
    for layer in reversed(range(layer_count)):
        if received is None:
            cot, send = pl.pallas_call(
                partial(first_dual_kernel, layer),
                out_shape=(dual_shape, message),
                in_specs=[SMEM] + [VMEM] * 3,
                out_specs=(VMEM, VMEM),
                compiler_params=PARAMS,
            )(index, cot, dual_active, saved_dual)
        else:
            cot, send, terms = pl.pallas_call(
                partial(dual_kernel, layer),
                out_shape=(dual_shape, message, terms_shape),
                in_specs=[SMEM] + [VMEM] * 4,
                out_specs=(VMEM,) * 3,
                compiler_params=PARAMS,
            )(index, received, cot, dual_active, saved_dual)
            all_terms.append(terms)
        fetched = exchange(send)
        mine = pl.pallas_call(
            pull_kernel,
            out_shape=jax.ShapeDtypeStruct((primal_count, 2 * channels, side), F32),
            in_specs=[SMEM] + [VMEM] * 2,
            out_specs=VMEM,
            compiler_params=PARAMS,
        )(index, tile_blocks, fetched)
        other = lax.ppermute(mine, "col", swap)
        grad_x, push = pl.pallas_call(
            partial(primal_kernel, layer),
            out_shape=(jax.ShapeDtypeStruct(cot_primal.shape, F32), message),
            in_specs=[SMEM] * 2 + [VMEM] * 8,
            out_specs=(VMEM, VMEM),
            scratch_shapes=[pltpu.VMEM(cot_primal.shape, BF16)],
            compiler_params=PARAMS,
        )(
            index,
            steps,
            tile_blocks,
            mine,
            other,
            grad_x,
            primal_active,
            saved_primal,
            dual_mix,
            primal_mix,
        )
        received = exchange(push)
    grad_y, terms = pl.pallas_call(
        last_dual_kernel,
        out_shape=(dual_shape, terms_shape),
        in_specs=[SMEM] + [VMEM] * 2,
        out_specs=(VMEM, VMEM),
        compiler_params=PARAMS,
    )(index, received, cot)
    all_terms.append(terms)
    terms = jnp.stack(all_terms[::-1])
    dual_mix_grad = (-row_scale * steps[:, 1])[:, None, None] * terms[:, :, :channels]
    primal_mix_grad = (-col_scale * steps[:, 0])[:, None, None] * terms[
        :, :, channels : 2 * channels
    ]
    return (grad_x, grad_y, primal_mix_grad, dual_mix_grad)


def solution(mesh):
    return jax.shard_map(
        per_device,
        mesh=mesh,
        in_specs=(
            P(("groups", "row", "col"), None, None),
            P(("groups", "row", "col")),
            P(("groups", "row", "col")),
            P(None, ("groups", "row"), None, None),
            P(None, ("groups", "row", "col"), None, None),
            P(None, ("groups", "row"), None),
            P(None, ("groups", "row", "col"), None),
            P(),
            P(),
            P(),
            P(("groups", "row"), None, None),
            P(("groups", "row", "col"), None, None),
        ),
        out_specs=(
            P(("groups", "row"), None, None),
            P(("groups", "row", "col"), None, None),
            P("groups", None, None),
            P("groups", None, None),
        ),
        check_vma=False,
    )
```

```python
from functools import partial
import math

import jax
import jax.numpy as jnp
from jax import lax
from jax.experimental import pallas as pl
from jax.experimental.pallas import tpu as pltpu
from jax.sharding import PartitionSpec as P

SMEM = pl.BlockSpec(memory_space=pltpu.SMEM)
VMEM = pl.BlockSpec(memory_space=pltpu.VMEM)
F32 = jnp.float32
BF16 = jnp.bfloat16


def loop(count, body):
    if count <= 16:
        for i in range(count):
            body(i)
    else:
        lax.fori_loop(0, count, lambda i, _: (body(i), 0)[1], 0)


def total_of(count, term, shape):
    if count <= 16:
        total = term(0)
        for i in range(1, count):
            total = total + term(i)
        return total
    return lax.fori_loop(0, count, lambda i, t: t + term(i), jnp.zeros(shape, F32))


def halves(x):
    high = x.astype(BF16)
    return high, (x - high.astype(F32)).astype(BF16)


def prepare_kernel(
    peer_size,
    primal_count,
    rows_ref,
    cols_ref,
    steps_ref,
    tiles_in,
    cot_in,
    mask_ref,
    saved_ref,
    dual_mix_ref,
    primal_mix_ref,
    tiles_ref,
    place_ref,
    scale_ref,
    mix_ref,
    cot_ref,
    base_ref,
    pad_ref,
):
    owned, channels, side = cot_ref.shape
    layers = dual_mix_ref.shape[0]

    def one(t):
        peer = lax.div(rows_ref[t], peer_size)
        tiles_ref[peer] = tiles_in[t]
        p = lax.rem(cols_ref[t], primal_count)
        place_ref[peer] = jnp.full(place_ref.shape[1:], p.astype(F32), F32)

    loop(tiles_ref.shape[0], one)
    for k in range(layers):
        for s in range(2):
            upper = jnp.full((1, side), steps_ref[k, 2 * s].astype(F32), F32)
            lower = jnp.full((1, side), steps_ref[k, 2 * s + 1].astype(F32), F32)
            scale_ref[pl.ds(2 * k + s, 1), :] = -(upper / lower)
    pad_ref[...] = jnp.zeros_like(pad_ref)
    for k in range(layers):
        for s, ref in enumerate((primal_mix_ref, dual_mix_ref)):
            pad_ref[:, :channels] = ref[k]
            weights = pad_ref[...]
            high = weights.astype(BF16).astype(F32)
            rest = weights - high
            mix_ref[2 * k + s] = (
                high
                + pltpu.roll(high, channels, 1)
                + pltpu.roll(rest, 2 * channels, 1)
                + pltpu.roll(rest, 3 * channels, 1)
            ).astype(BF16)
    for b in range(owned):
        cot = mask_ref[layers - 1, pl.ds(b, 1), :].astype(F32) * cot_in[b]
        cot_ref[b] = cot
        base_ref[b, :channels, :] = cot.astype(BF16)
        base_ref[b, channels:, :] = saved_ref[layers - 1, b]


def choose(place_ref, base, send_ref):
    copies = base[0].shape[0] // place_ref.shape[1]

    def one(r):
        place = jnp.concatenate([place_ref[r]] * copies, 0)
        picked = base[0]
        for b in range(1, len(base)):
            picked = jnp.where(place == b, base[b], picked)
        send_ref[r] = picked.astype(BF16)

    loop(send_ref.shape[0], one)


def first_dual_kernel(wanted_ref, base_ref, send_ref):
    owned = base_ref.shape[0]
    choose(wanted_ref, [base_ref[b].astype(F32) for b in range(owned)], send_ref)


def add_pushed(wanted_ref, received_ref, cot_ref):
    owned, channels, side = cot_ref.shape
    rows = received_ref.shape[0]
    copies = channels // wanted_ref.shape[1]
    place = lambda r: jnp.concatenate([wanted_ref[r]] * copies, 0)
    if rows <= 16:
        blocks = [cot_ref[b] for b in range(owned)]
        for r in range(rows):
            at, pushed = place(r), received_ref[r, :channels, :].astype(F32)
            blocks = [block + jnp.where(at == b, pushed, 0.0) for b, block in enumerate(blocks)]
        return blocks

    def step(r, blocks):
        at, pushed = place(r), received_ref[r, :channels, :].astype(F32)
        return tuple(block + jnp.where(at == b, pushed, 0.0) for b, block in enumerate(blocks))

    return list(lax.fori_loop(0, rows, step, tuple(cot_ref[b] for b in range(owned))))


def sum_terms(received_ref):
    rows, height, side = received_ref.shape
    channels = height // 2
    return total_of(
        rows, lambda r: received_ref[r, channels:, :].astype(F32), (channels, side)
    )


def dual_kernel(
    layer, wanted_ref, received_ref, cot_in, mask_ref, saved_ref, cot_ref, send_ref, terms_ref
):
    base = []
    for b, block in enumerate(add_pushed(wanted_ref, received_ref, cot_in)):
        cot = mask_ref[layer, pl.ds(b, 1), :].astype(F32) * block
        cot_ref[b] = cot
        base.append(jnp.concatenate([cot, saved_ref[layer, b].astype(F32)], 0))
    choose(wanted_ref, base, send_ref)
    terms_ref[...] = sum_terms(received_ref)


def last_dual_kernel(
    row_scale, col_scale, wanted_ref, received_ref, cot_in, scale_ref, *refs
):
    terms_refs, (cot_ref, primal_ref, dual_ref) = refs[:-3], refs[-3:]
    channels = cot_ref.shape[1]
    layers = primal_ref.shape[0]
    for b, block in enumerate(add_pushed(wanted_ref, received_ref, cot_in)):
        cot_ref[b] = block
    for k in range(layers):
        terms = sum_terms(received_ref) if k == 0 else terms_refs[k - 1][...]
        side = terms.shape[1]
        terms = terms + pltpu.roll(terms, side - channels, 1)
        dual = scale_ref[pl.ds(2 * k + 1, 1), :] * row_scale * terms
        primal = scale_ref[pl.ds(2 * k, 1), :] * col_scale * terms
        dual_ref[k] = dual[:, :channels]
        primal_ref[k] = pltpu.roll(primal, side - 2 * channels, 1)[:, :channels]


def pull_kernel(tiles_ref, place_ref, received_ref, sum_ref):
    count = sum_ref.shape[0]
    rows = tiles_ref.shape[0]
    copies = received_ref.shape[1] // place_ref.shape[1]

    def step(t, sums):
        product = jnp.dot(received_ref[t], tiles_ref[t], preferred_element_type=F32)
        at = jnp.concatenate([place_ref[t]] * copies, 0)
        return tuple(s + jnp.where(at == p, product, 0.0) for p, s in enumerate(sums))

    sums = tuple(jnp.zeros(sum_ref.shape[1:], F32) for _ in range(count))
    if rows <= 16:
        for t in range(rows):
            sums = step(t, sums)
    else:
        sums = lax.fori_loop(0, rows, step, sums)
    for p in range(count):
        sum_ref[p] = sums[p]


def primal_kernel(
    layer,
    tiles_ref,
    place_ref,
    scale_ref,
    mix_ref,
    mine_ref,
    other_ref,
    grad_in,
    mask_ref,
    saved_ref,
    grad_ref,
    send_ref,
):
    blocks, channels, side = grad_ref.shape
    sigma = scale_ref[pl.ds(2 * layer + 1, 1), :]
    tau = scale_ref[pl.ds(2 * layer, 1), :]

    def mix(weights, x):
        high, rest = halves(x)
        return jnp.dot(
            weights, jnp.concatenate([high, rest, high, rest], 0), preferred_element_type=F32
        )

    mixed, left, right = [], [], []
    for p in range(blocks):
        both = mine_ref[p] + other_ref[p]
        pulled_mixed, pulled_saved = both[:channels], both[channels:]
        back = sigma * mix(mix_ref[2 * layer + 1], pulled_mixed)
        primal_cot = mask_ref[layer, pl.ds(p, 1), :].astype(F32) * (grad_in[p] + 2.0 * back)
        grad_ref[p] = primal_cot - back
        mixed.append((tau * mix(mix_ref[2 * layer], primal_cot)).astype(BF16).astype(F32))
        extrapolated = (
            2.0 * saved_ref[layer + 1, p].astype(F32) - saved_ref[layer, p].astype(F32)
        ).astype(BF16)
        left.append(jnp.concatenate([extrapolated, *halves(pulled_saved)], 0))
        right.append(jnp.concatenate([*halves(pulled_mixed), *halves(primal_cot)], 0))
    terms = lax.dot_general(
        jnp.concatenate(left, 1),
        jnp.concatenate(right, 1),
        (((1,), (1,)), ((), ())),
        preferred_element_type=F32,
    )
    lane = lax.broadcasted_iota(jnp.int32, (channels, side), 1)
    terms = jnp.where(
        lane < 2 * channels,
        terms[:channels],
        terms[channels : 2 * channels] + terms[2 * channels :],
    )
    terms = terms + pltpu.roll(terms, side - channels, 1)
    high = terms.astype(BF16).astype(F32)
    rest = pltpu.roll(terms - high, channels, 1)
    packed = jnp.where(lax.rem(lane, 2 * channels) < channels, high, rest).astype(BF16)
    copies = channels // place_ref.shape[1]

    def one(t):
        at = jnp.concatenate([place_ref[t]] * copies, 0)
        picked = mixed[0]
        for p in range(1, blocks):
            picked = jnp.where(at == p, mixed[p], picked)
        product = lax.dot_general(
            picked.astype(BF16),
            tiles_ref[t],
            (((1,), (1,)), ((), ())),
            preferred_element_type=F32,
        )
        send_ref[t, :channels, :] = product.astype(BF16)
        send_ref[t, channels:, :] = packed

    loop(tiles_ref.shape[0], one)


def per_device(
    tile_blocks,
    tile_rows,
    tile_cols,
    saved_primal,
    saved_dual,
    primal_active,
    dual_active,
    primal_mix,
    dual_mix,
    step_fracs,
    cot_primal,
    cot_dual,
):
    row_count = lax.axis_size("row")
    col_count = lax.axis_size("col")
    owned, channels, side = cot_dual.shape
    primal_count = cot_primal.shape[0]
    layer_count = primal_mix.shape[0]
    row_scale = 1.0 / math.sqrt(owned * row_count * col_count * side)
    col_scale = 1.0 / math.sqrt(primal_count * row_count * side)
    params = pltpu.CompilerParams(vmem_limit_bytes=16 * 1024 * 1024)

    def call(kernel, outs, *operands, smem=0, **rest):
        return pl.pallas_call(
            kernel,
            out_shape=outs,
            in_specs=[SMEM] * smem + [VMEM] * (len(operands) - smem),
            out_specs=jax.tree.map(lambda _: VMEM, outs),
            compiler_params=params,
            **rest,
        )(*operands)

    def exchange(x):
        return lax.all_to_all(x, "row", split_axis=0, concat_axis=0, tiled=True)

    def shape(dims, kind=F32):
        return jax.ShapeDtypeStruct(dims, kind)

    peers = tile_rows // (owned * col_count)
    peer_ids = jnp.arange(row_count, dtype=jnp.int32)
    asked = jnp.sum(
        jnp.where(peers[None, :] == peer_ids[:, None], (tile_rows % owned)[None, :], 0), axis=1
    )
    wanted = exchange(
        jnp.broadcast_to(asked.astype(F32)[:, None, None], (row_count, 8, side))
    )
    message = shape((row_count, 2 * channels, side), BF16)
    tiles, place, scale, mix, cot, base = call(
        partial(prepare_kernel, owned * col_count, primal_count),
        (
            shape(tile_blocks.shape, BF16),
            shape((row_count, 8, side)),
            shape((2 * layer_count, side)),
            shape((2 * layer_count, channels, side), BF16),
            shape(cot_dual.shape),
            shape((owned, 2 * channels, side), BF16),
        ),
        tile_rows,
        tile_cols,
        step_fracs,
        tile_blocks,
        cot_dual,
        dual_active,
        saved_dual,
        dual_mix,
        primal_mix,
        smem=3,
        scratch_shapes=[pltpu.VMEM((channels, side), F32)],
    )
    swap = [(i, col_count - 1 - i) for i in range(col_count)]
    grad_x = cot_primal
    received = None
    all_terms = []
    for layer in reversed(range(layer_count)):
        if received is None:
            send = call(first_dual_kernel, message, wanted, base)
        else:
            cot, send, terms = call(
                partial(dual_kernel, layer),
                (shape(cot_dual.shape), message, shape((channels, side))),
                wanted,
                received,
                cot,
                dual_active,
                saved_dual,
            )
            all_terms.insert(0, terms)
        fetched = exchange(send)
        mine = call(
            pull_kernel, shape((primal_count, 2 * channels, side)), tiles, place, fetched
        )
        other = lax.ppermute(mine, "col", swap)
        grad_x, push = call(
            partial(primal_kernel, layer),
            (shape(cot_primal.shape), message),
            tiles,
            place,
            scale,
            mix,
            mine,
            other,
            grad_x,
            primal_active,
            saved_primal,
        )
        received = exchange(push)
    grad_y, primal_mix_grad, dual_mix_grad = call(
        partial(last_dual_kernel, row_scale, col_scale),
        (shape(cot_dual.shape), shape(primal_mix.shape), shape(dual_mix.shape)),
        wanted,
        received,
        cot,
        scale,
        *all_terms,
    )
    return (grad_x, grad_y, primal_mix_grad, dual_mix_grad)


def solution(mesh):
    return jax.shard_map(
        per_device,
        mesh=mesh,
        in_specs=(
            P(("groups", "row", "col"), None, None),
            P(("groups", "row", "col")),
            P(("groups", "row", "col")),
            P(None, ("groups", "row"), None, None),
            P(None, ("groups", "row", "col"), None, None),
            P(None, ("groups", "row"), None),
            P(None, ("groups", "row", "col"), None),
            P(),
            P(),
            P(),
            P(("groups", "row"), None, None),
            P(("groups", "row", "col"), None, None),
        ),
        out_specs=(
            P(("groups", "row"), None, None),
            P(("groups", "row", "col"), None, None),
            P("groups", None, None),
            P("groups", None, None),
        ),
        check_vma=False,
    )
```

```python
from functools import partial
import math

import jax
import jax.numpy as jnp
from jax import lax
from jax.experimental import pallas as pl
from jax.experimental.pallas import tpu as pltpu
from jax.sharding import PartitionSpec as P

SMEM = pl.BlockSpec(memory_space=pltpu.SMEM)
VMEM = pl.BlockSpec(memory_space=pltpu.VMEM)
HBM = pl.BlockSpec(memory_space=pltpu.HBM)
F32 = jnp.float32
BF16 = jnp.bfloat16


def loop(count, body):
    if count <= 16:
        for i in range(count):
            body(i)
    else:
        lax.fori_loop(0, count, lambda i, _: (body(i), 0)[1], 0)


def total_of(count, term, shape):
    if count <= 16:
        total = term(0)
        for i in range(1, count):
            total = total + term(i)
        return total
    return lax.fori_loop(0, count, lambda i, t: t + term(i), jnp.zeros(shape, F32))


def halves(x):
    high = x.astype(BF16)
    return high, (x - high.astype(F32)).astype(BF16)


def prepare_kernel(
    peer_size,
    primal_count,
    rows_ref,
    cols_ref,
    steps_ref,
    tiles_in,
    cot_in,
    mask_in,
    saved_in,
    dual_mix_in,
    primal_mix_in,
    tiles_ref,
    place_ref,
    scale_ref,
    mix_ref,
    cot_ref,
    base_ref,
    pad_ref,
    mask_ref,
    saved_ref,
    mixes_ref,
    sems,
    tile_sems,
):
    owned, channels, side = cot_ref.shape
    layers = dual_mix_in.shape[0]
    fetches = [
        pltpu.make_async_copy(source, target, sems.at[i])
        for i, (source, target) in enumerate(
            (
                (cot_in, cot_ref),
                (saved_in.at[layers - 1], saved_ref),
                (mask_in.at[layers - 1], mask_ref),
                (primal_mix_in, mixes_ref.at[0]),
                (dual_mix_in, mixes_ref.at[1]),
            )
        )
    ]
    for fetch in fetches:
        fetch.start()

    def fetch_tile(t):
        peer = lax.div(rows_ref[t], peer_size)
        return pltpu.make_async_copy(tiles_in.at[t], tiles_ref.at[peer], tile_sems.at[t])

    loop(tiles_ref.shape[0], lambda t: fetch_tile(t).start())

    def one(t):
        p = lax.rem(cols_ref[t], primal_count)
        filled = jnp.full(place_ref.shape[1:], p.astype(F32), F32)
        place_ref[lax.div(rows_ref[t], peer_size)] = filled

    loop(tiles_ref.shape[0], one)
    for k in range(layers):
        for s in range(2):
            upper = jnp.full((1, side), steps_ref[k, 2 * s].astype(F32), F32)
            lower = jnp.full((1, side), steps_ref[k, 2 * s + 1].astype(F32), F32)
            scale_ref[pl.ds(2 * k + s, 1), :] = -(upper / lower)
    pad_ref[...] = jnp.zeros_like(pad_ref)
    for fetch in fetches:
        fetch.wait()
    for b in range(owned):
        cot = mask_ref[pl.ds(b, 1), :].astype(F32) * cot_ref[b]
        cot_ref[b] = cot
        base_ref[b, :channels, :] = cot.astype(BF16)
        base_ref[b, channels:, :] = saved_ref[b]
    for k in range(layers):
        for s in range(2):
            pad_ref[2 * k + s, :, :channels] = mixes_ref[s, k]
            weights = pad_ref[2 * k + s]
            high = weights.astype(BF16).astype(F32)
            rest = weights - high
            mix_ref[2 * k + s] = (
                high
                + pltpu.roll(high, channels, 1)
                + pltpu.roll(rest, 2 * channels, 1)
                + pltpu.roll(rest, 3 * channels, 1)
            ).astype(BF16)
    loop(tiles_ref.shape[0], lambda t: fetch_tile(t).wait())


def choose(place_ref, base, send_ref):
    copies = base[0].shape[0] // place_ref.shape[1]

    def one(r):
        place = jnp.concatenate([place_ref[r]] * copies, 0)
        picked = base[0]
        for b in range(1, len(base)):
            picked = jnp.where(place == b, base[b], picked)
        send_ref[r] = picked.astype(BF16)

    loop(send_ref.shape[0], one)


def first_dual_kernel(wanted_ref, base_ref, send_ref):
    owned = base_ref.shape[0]
    choose(wanted_ref, [base_ref[b].astype(F32) for b in range(owned)], send_ref)


def add_pushed(wanted_ref, received_ref, cot_ref):
    owned, channels, side = cot_ref.shape
    rows = received_ref.shape[0]
    copies = channels // wanted_ref.shape[1]
    place = lambda r: jnp.concatenate([wanted_ref[r]] * copies, 0)
    if rows <= 16:
        blocks = [cot_ref[b] for b in range(owned)]
        for r in range(rows):
            at, pushed = place(r), received_ref[r, :channels, :].astype(F32)
            blocks = [block + jnp.where(at == b, pushed, 0.0) for b, block in enumerate(blocks)]
        return blocks

    def step(r, blocks):
        at, pushed = place(r), received_ref[r, :channels, :].astype(F32)
        return tuple(block + jnp.where(at == b, pushed, 0.0) for b, block in enumerate(blocks))

    return list(lax.fori_loop(0, rows, step, tuple(cot_ref[b] for b in range(owned))))


def sum_terms(received_ref, channels):
    rows, height, side = received_ref.shape
    return total_of(
        rows, lambda r: received_ref[r, channels:, :].astype(F32), (height - channels, side)
    )


def dual_kernel(
    layer, wanted_ref, received_ref, cot_in, mask_ref, saved_ref, cot_ref, send_ref, terms_ref
):
    base = []
    for b, block in enumerate(add_pushed(wanted_ref, received_ref, cot_in)):
        cot = mask_ref[layer, pl.ds(b, 1), :].astype(F32) * block
        cot_ref[b] = cot
        base.append(jnp.concatenate([cot, saved_ref[layer, b].astype(F32)], 0))
    choose(wanted_ref, base, send_ref)
    terms_ref[...] = sum_terms(received_ref, cot_ref.shape[1])


def last_dual_kernel(
    row_scale, col_scale, wanted_ref, received_ref, cot_in, scale_ref, grad_in, *refs
):
    terms_refs, refs = refs[:-8], refs[-8:]
    grad_ref, cot_ref, primal_out, dual_out, held_ref, primal_ref, dual_ref, sems = refs
    owned, channels, side = held_ref.shape
    layers = primal_ref.shape[0]
    copies = [pltpu.make_async_copy(grad_in, grad_ref, sems.at[owned])]
    copies[0].start()
    for b, block in enumerate(add_pushed(wanted_ref, received_ref, cot_in)):
        held_ref[b] = block
        copy = pltpu.make_async_copy(held_ref.at[b], cot_ref.at[b], sems.at[b])
        copy.start()
        copies.append(copy)
    for k in range(layers):
        terms = sum_terms(received_ref, channels) if k == 0 else terms_refs[k - 1][...]
        half = terms.shape[0]
        dual = scale_ref[pl.ds(2 * k + 1, 1), :] * row_scale * terms
        primal = scale_ref[pl.ds(2 * k, 1), :] * col_scale * terms
        dual_ref[k, :half, :] = dual[:, :channels]
        dual_ref[k, half:, :] = pltpu.roll(dual, side - channels, 1)[:, :channels]
        primal_ref[k, :half, :] = pltpu.roll(primal, side - 2 * channels, 1)[:, :channels]
        primal_ref[k, half:, :] = pltpu.roll(primal, side - 3 * channels, 1)[:, :channels]
    for i, (source, target) in enumerate(((primal_ref, primal_out), (dual_ref, dual_out))):
        copies.append(pltpu.make_async_copy(source, target, sems.at[owned + 1 + i]))
        copies[-1].start()
    for copy in copies:
        copy.wait()


def pull_kernel(tiles_ref, place_ref, received_ref, sum_ref):
    count = sum_ref.shape[0]
    rows = tiles_ref.shape[0]
    copies = received_ref.shape[1] // place_ref.shape[1]

    def step(t, sums):
        product = jnp.dot(received_ref[t], tiles_ref[t], preferred_element_type=F32)
        at = jnp.concatenate([place_ref[t]] * copies, 0)
        return tuple(s + jnp.where(at == p, product, 0.0) for p, s in enumerate(sums))

    sums = tuple(jnp.zeros(sum_ref.shape[1:], F32) for _ in range(count))
    if rows <= 16:
        for t in range(rows):
            sums = step(t, sums)
    else:
        sums = lax.fori_loop(0, rows, step, sums)
    for p in range(count):
        sum_ref[p] = sums[p]


def primal_kernel(
    layer,
    tiles_ref,
    place_ref,
    scale_ref,
    mix_ref,
    mine_ref,
    other_ref,
    grad_in,
    mask_ref,
    saved_ref,
    grad_ref,
    send_ref,
):
    blocks, channels, side = grad_ref.shape
    sigma = scale_ref[pl.ds(2 * layer + 1, 1), :]
    tau = scale_ref[pl.ds(2 * layer, 1), :]

    def mix(weights, x):
        high, rest = halves(x)
        return jnp.dot(
            weights, jnp.concatenate([high, rest, high, rest], 0), preferred_element_type=F32
        )

    mixed, left, right = [], [], []
    for p in range(blocks):
        both = mine_ref[p] + other_ref[p]
        pulled_mixed, pulled_saved = both[:channels], both[channels:]
        back = sigma * mix(mix_ref[2 * layer + 1], pulled_mixed)
        primal_cot = mask_ref[layer, pl.ds(p, 1), :].astype(F32) * (grad_in[p] + 2.0 * back)
        grad_ref[p] = primal_cot - back
        mixed.append((tau * mix(mix_ref[2 * layer], primal_cot)).astype(BF16).astype(F32))
        extrapolated = (
            2.0 * saved_ref[layer + 1, p].astype(F32) - saved_ref[layer, p].astype(F32)
        ).astype(BF16)
        left.append(jnp.concatenate([extrapolated, *halves(pulled_saved)], 0))
        right.append(jnp.concatenate([*halves(pulled_mixed), *halves(primal_cot)], 0))
    terms = lax.dot_general(
        jnp.concatenate(left, 1),
        jnp.concatenate(right, 1),
        (((1,), (1,)), ((), ())),
        preferred_element_type=F32,
    )
    lane = lax.broadcasted_iota(jnp.int32, (channels, side), 1)
    terms = jnp.where(
        lane < 2 * channels,
        terms[:channels],
        terms[channels : 2 * channels] + terms[2 * channels :],
    )
    terms = terms + pltpu.roll(terms, side - channels, 1)
    half = channels // 2
    packed = jnp.where(
        lax.rem(lane[:half], 2 * channels) < channels,
        terms[:half],
        pltpu.roll(terms[half:], channels, 1),
    ).astype(BF16)
    copies = channels // place_ref.shape[1]

    def one(t):
        at = jnp.concatenate([place_ref[t]] * copies, 0)
        picked = mixed[0]
        for p in range(1, blocks):
            picked = jnp.where(at == p, mixed[p], picked)
        product = lax.dot_general(
            picked.astype(BF16),
            tiles_ref[t],
            (((1,), (1,)), ((), ())),
            preferred_element_type=F32,
        )
        send_ref[t, :channels, :] = product.astype(BF16)
        send_ref[t, channels:, :] = packed

    loop(tiles_ref.shape[0], one)


def per_device(
    tile_blocks,
    tile_rows,
    tile_cols,
    saved_primal,
    saved_dual,
    primal_active,
    dual_active,
    primal_mix,
    dual_mix,
    step_fracs,
    cot_primal,
    cot_dual,
):
    row_count = lax.axis_size("row")
    col_count = lax.axis_size("col")
    owned, channels, side = cot_dual.shape
    primal_count = cot_primal.shape[0]
    layer_count = primal_mix.shape[0]
    row_scale = 1.0 / math.sqrt(owned * row_count * col_count * side)
    col_scale = 1.0 / math.sqrt(primal_count * row_count * side)
    params = pltpu.CompilerParams(vmem_limit_bytes=16 * 1024 * 1024)

    def call(kernel, outs, *operands, ins=None, out_specs=None, **rest):
        return pl.pallas_call(
            kernel,
            out_shape=outs,
            in_specs=ins or [VMEM] * len(operands),
            out_specs=out_specs or jax.tree.map(lambda _: VMEM, outs),
            compiler_params=params,
            **rest,
        )(*operands)

    def exchange(x):
        return lax.all_to_all(x, "row", split_axis=0, concat_axis=0, tiled=True)

    def shape(dims, kind=F32):
        return jax.ShapeDtypeStruct(dims, kind)

    peers = tile_rows // (owned * col_count)
    peer_ids = jnp.arange(row_count, dtype=jnp.int32)
    asked = jnp.sum(
        jnp.where(peers[None, :] == peer_ids[:, None], (tile_rows % owned)[None, :], 0), axis=1
    )
    wanted = exchange(
        jnp.broadcast_to(asked.astype(F32)[:, None, None], (row_count, 8, side))
    )
    message = shape((row_count, 2 * channels, side), BF16)
    pushed = shape((row_count, channels + channels // 2, side), BF16)
    terms_shape = shape((channels // 2, side))
    tiles, place, scale, mix, cot, base = call(
        partial(prepare_kernel, owned * col_count, primal_count),
        (
            shape(tile_blocks.shape, BF16),
            shape((row_count, 8, side)),
            shape((2 * layer_count, side)),
            shape((2 * layer_count, channels, side), BF16),
            shape(cot_dual.shape),
            shape((owned, 2 * channels, side), BF16),
        ),
        tile_rows,
        tile_cols,
        step_fracs,
        *(
            pltpu.with_memory_space_constraint(x, pltpu.HBM)
            for x in (tile_blocks, cot_dual, dual_active, saved_dual, dual_mix, primal_mix)
        ),
        ins=[SMEM] * 3 + [HBM] * 6,
        scratch_shapes=[
            pltpu.VMEM((2 * layer_count, channels, side), F32),
            pltpu.VMEM((owned, side), jnp.int32),
            pltpu.VMEM((owned, channels, side), BF16),
            pltpu.VMEM((2, layer_count, channels, channels), F32),
            pltpu.SemaphoreType.DMA((5,)),
            pltpu.SemaphoreType.DMA((row_count,)),
        ],
    )
    swap = [(i, col_count - 1 - i) for i in range(col_count)]
    grad_x = cot_primal
    received = None
    all_terms = []
    for layer in reversed(range(layer_count)):
        if received is None:
            send = call(first_dual_kernel, message, wanted, base)
        else:
            cot, send, terms = call(
                partial(dual_kernel, layer),
                (shape(cot_dual.shape), message, terms_shape),
                wanted,
                received,
                cot,
                dual_active,
                saved_dual,
            )
            all_terms.insert(0, terms)
        fetched = exchange(send)
        mine = call(
            pull_kernel, shape((primal_count, 2 * channels, side)), tiles, place, fetched
        )
        other = lax.ppermute(mine, "col", swap)
        grad_x, push = call(
            partial(primal_kernel, layer),
            (shape(cot_primal.shape), pushed),
            tiles,
            place,
            scale,
            mix,
            mine,
            other,
            grad_x,
            primal_active,
            saved_primal,
        )
        received = exchange(push)
    grad_x, grad_y, primal_mix_grad, dual_mix_grad = call(
        partial(last_dual_kernel, row_scale, col_scale),
        (
            shape(cot_primal.shape),
            shape(cot_dual.shape),
            shape(primal_mix.shape),
            shape(dual_mix.shape),
        ),
        wanted,
        received,
        cot,
        scale,
        grad_x,
        *all_terms,
        out_specs=(HBM,) * 4,
        scratch_shapes=[
            pltpu.VMEM(cot_dual.shape, F32),
            pltpu.VMEM(primal_mix.shape, F32),
            pltpu.VMEM(dual_mix.shape, F32),
            pltpu.SemaphoreType.DMA((owned + 3,)),
        ],
    )
    return (grad_x, grad_y, primal_mix_grad, dual_mix_grad)


def solution(mesh):
    return jax.shard_map(
        per_device,
        mesh=mesh,
        in_specs=(
            P(("groups", "row", "col"), None, None),
            P(("groups", "row", "col")),
            P(("groups", "row", "col")),
            P(None, ("groups", "row"), None, None),
            P(None, ("groups", "row", "col"), None, None),
            P(None, ("groups", "row"), None),
            P(None, ("groups", "row", "col"), None),
            P(),
            P(),
            P(),
            P(("groups", "row"), None, None),
            P(("groups", "row", "col"), None, None),
        ),
        out_specs=(
            P(("groups", "row"), None, None),
            P(("groups", "row", "col"), None, None),
            P("groups", None, None),
            P("groups", None, None),
        ),
        check_vma=False,
    )
```

```python
from functools import partial
import math

import jax
import jax.numpy as jnp
from jax import lax
from jax.experimental import pallas as pl
from jax.experimental.pallas import tpu as pltpu
from jax.sharding import PartitionSpec as P

VMEM = pl.BlockSpec(memory_space=pltpu.VMEM)
HBM = pl.BlockSpec(memory_space=pltpu.HBM)
F32 = jnp.float32
BF16 = jnp.bfloat16


def loop(count, body):
    if count <= 16:
        for i in range(count):
            body(i)
    else:
        lax.fori_loop(0, count, lambda i, _: (body(i), 0)[1], 0)


def total_of(count, term, shape):
    if count <= 16:
        total = term(0)
        for i in range(1, count):
            total = total + term(i)
        return total
    return lax.fori_loop(0, count, lambda i, t: t + term(i), jnp.zeros(shape, F32))


def halves(x):
    high = x.astype(BF16)
    return high, (x - high.astype(F32)).astype(BF16)


def ask_kernel(peer_size, owned, rows_in, asked_ref, rows_ref, sem):
    fetch = pltpu.make_async_copy(rows_in, rows_ref, sem)
    fetch.start()
    fetch.wait()

    def one(t):
        place = lax.rem(rows_ref[t], owned)
        filled = jnp.full(asked_ref.shape[1:], place.astype(F32), F32)
        asked_ref[lax.div(rows_ref[t], peer_size)] = filled

    loop(asked_ref.shape[0], one)


def prepare_kernel(
    peer_size,
    primal_count,
    rows_in,
    cols_in,
    steps_in,
    tiles_in,
    cot_in,
    mask_in,
    saved_in,
    dual_mix_in,
    primal_mix_in,
    tiles_ref,
    place_ref,
    scale_ref,
    mix_ref,
    cot_ref,
    base_ref,
    pad_ref,
    rows_ref,
    cols_ref,
    steps_ref,
    mask_ref,
    saved_ref,
    mixes_ref,
    held_ref,
    sems,
):
    owned, channels, side = cot_ref.shape
    layers = dual_mix_in.shape[0]
    fetches = [
        pltpu.make_async_copy(source, target, sems.at[i])
        for i, (source, target) in enumerate(
            (
                (rows_in, rows_ref),
                (cols_in, cols_ref),
                (steps_in, steps_ref),
                (tiles_in, held_ref),
                (cot_in, cot_ref),
                (saved_in.at[layers - 1], saved_ref),
                (mask_in.at[layers - 1], mask_ref),
                (primal_mix_in, mixes_ref.at[0]),
                (dual_mix_in, mixes_ref.at[1]),
            )
        )
    ]
    for fetch in fetches:
        fetch.start()
    pad_ref[...] = jnp.zeros_like(pad_ref)
    for fetch in fetches[:3]:
        fetch.wait()

    def one(t):
        p = lax.rem(cols_ref[t], primal_count)
        filled = jnp.full(place_ref.shape[1:], p.astype(F32), F32)
        place_ref[lax.div(rows_ref[t], peer_size)] = filled

    loop(tiles_ref.shape[0], one)
    for k in range(layers):
        for s in range(2):
            upper = jnp.full((1, side), steps_ref[k, 2 * s].astype(F32), F32)
            lower = jnp.full((1, side), steps_ref[k, 2 * s + 1].astype(F32), F32)
            scale_ref[pl.ds(2 * k + s, 1), :] = -(upper / lower)
    for fetch in fetches[7:]:
        fetch.wait()
    for k in range(layers):
        for s in range(2):
            pad_ref[2 * k + s, :, :channels] = mixes_ref[s, k]
            weights = pad_ref[2 * k + s]
            high = weights.astype(BF16).astype(F32)
            rest = weights - high
            mix_ref[2 * k + s] = (
                high
                + pltpu.roll(high, channels, 1)
                + pltpu.roll(rest, 2 * channels, 1)
                + pltpu.roll(rest, 3 * channels, 1)
            ).astype(BF16)
    for fetch in fetches[4:7]:
        fetch.wait()
    for b in range(owned):
        cot = mask_ref[pl.ds(b, 1), :].astype(F32) * cot_ref[b]
        cot_ref[b] = cot
        base_ref[b, :channels, :] = cot.astype(BF16)
        base_ref[b, channels:, :] = saved_ref[b]
    fetches[3].wait()

    def sort(t):
        tiles_ref[lax.div(rows_ref[t], peer_size)] = held_ref[t]

    loop(tiles_ref.shape[0], sort)


def choose(place_ref, base, send_ref):
    def one(r):
        place = jnp.broadcast_to(place_ref[r], base[0].shape)
        picked = base[0]
        for b in range(1, len(base)):
            picked = jnp.where(place == b, base[b], picked)
        send_ref[r] = picked.astype(BF16)

    loop(send_ref.shape[0], one)


def first_dual_kernel(wanted_ref, base_ref, send_ref):
    owned = base_ref.shape[0]
    choose(wanted_ref, [base_ref[b].astype(F32) for b in range(owned)], send_ref)


def add_pushed(wanted_ref, received_ref, cot_ref):
    owned, channels, side = cot_ref.shape
    rows = received_ref.shape[0]
    place = lambda r: jnp.broadcast_to(wanted_ref[r], (channels, side))
    if rows <= 16:
        blocks = [cot_ref[b] for b in range(owned)]
        for r in range(rows):
            at, pushed = place(r), received_ref[r, :channels, :].astype(F32)
            blocks = [block + jnp.where(at == b, pushed, 0.0) for b, block in enumerate(blocks)]
        return blocks

    def step(r, blocks):
        at, pushed = place(r), received_ref[r, :channels, :].astype(F32)
        return tuple(block + jnp.where(at == b, pushed, 0.0) for b, block in enumerate(blocks))

    return list(lax.fori_loop(0, rows, step, tuple(cot_ref[b] for b in range(owned))))


def sum_terms(received_ref, channels):
    rows, height, side = received_ref.shape
    return total_of(
        rows, lambda r: received_ref[r, channels:, :].astype(F32), (height - channels, side)
    )


def dual_kernel(
    layer, wanted_ref, received_ref, cot_in, mask_ref, saved_ref, cot_ref, send_ref, terms_ref
):
    base = []
    for b, block in enumerate(add_pushed(wanted_ref, received_ref, cot_in)):
        cot = mask_ref[layer, pl.ds(b, 1), :].astype(F32) * block
        cot_ref[b] = cot
        base.append(jnp.concatenate([cot, saved_ref[layer, b].astype(F32)], 0))
    choose(wanted_ref, base, send_ref)
    terms_ref[...] = sum_terms(received_ref, cot_ref.shape[1])


def last_dual_kernel(
    row_scale, col_scale, wanted_ref, received_ref, cot_in, scale_ref, grad_in, *refs
):
    terms_refs, refs = refs[:-8], refs[-8:]
    grad_ref, cot_ref, primal_out, dual_out, held_ref, primal_ref, dual_ref, sems = refs
    owned, channels, side = held_ref.shape
    layers = primal_ref.shape[0]
    copies = [pltpu.make_async_copy(grad_in, grad_ref, sems.at[owned])]
    copies[0].start()
    for b, block in enumerate(add_pushed(wanted_ref, received_ref, cot_in)):
        held_ref[b] = block
        copy = pltpu.make_async_copy(held_ref.at[b], cot_ref.at[b], sems.at[b])
        copy.start()
        copies.append(copy)
    for k in range(layers):
        terms = sum_terms(received_ref, channels) if k == 0 else terms_refs[k - 1][...]
        half = terms.shape[0]
        dual = scale_ref[pl.ds(2 * k + 1, 1), :] * row_scale * terms
        primal = scale_ref[pl.ds(2 * k, 1), :] * col_scale * terms
        dual_ref[k, :half, :] = dual[:, :channels]
        dual_ref[k, half:, :] = pltpu.roll(dual, side - channels, 1)[:, :channels]
        primal_ref[k, :half, :] = pltpu.roll(primal, side - 2 * channels, 1)[:, :channels]
        primal_ref[k, half:, :] = pltpu.roll(primal, side - 3 * channels, 1)[:, :channels]
    for i, (source, target) in enumerate(((primal_ref, primal_out), (dual_ref, dual_out))):
        copies.append(pltpu.make_async_copy(source, target, sems.at[owned + 1 + i]))
        copies[-1].start()
    for copy in copies:
        copy.wait()


def pull_kernel(tiles_ref, place_ref, received_ref, sum_ref):
    count = sum_ref.shape[0]
    rows = tiles_ref.shape[0]

    def step(t, sums):
        product = jnp.dot(received_ref[t], tiles_ref[t], preferred_element_type=F32)
        at = jnp.broadcast_to(place_ref[t], product.shape)
        return tuple(s + jnp.where(at == p, product, 0.0) for p, s in enumerate(sums))

    sums = tuple(jnp.zeros(sum_ref.shape[1:], F32) for _ in range(count))
    if rows <= 16:
        for t in range(rows):
            sums = step(t, sums)
    else:
        sums = lax.fori_loop(0, rows, step, sums)
    for p in range(count):
        sum_ref[p] = sums[p]


def primal_kernel(
    layer,
    tiles_ref,
    place_ref,
    scale_ref,
    mix_ref,
    mine_ref,
    other_ref,
    grad_in,
    mask_ref,
    saved_ref,
    grad_ref,
    send_ref,
):
    blocks, channels, side = grad_ref.shape
    sigma = scale_ref[pl.ds(2 * layer + 1, 1), :]
    tau = scale_ref[pl.ds(2 * layer, 1), :]

    def mix(weights, x):
        high, rest = halves(x)
        return jnp.dot(
            weights, jnp.concatenate([high, rest, high, rest], 0), preferred_element_type=F32
        )

    mixed, left, right = [], [], []
    for p in range(blocks):
        both = mine_ref[p] + other_ref[p]
        pulled_mixed, pulled_saved = both[:channels], both[channels:]
        back = sigma * mix(mix_ref[2 * layer + 1], pulled_mixed)
        primal_cot = mask_ref[layer, pl.ds(p, 1), :].astype(F32) * (grad_in[p] + 2.0 * back)
        grad_ref[p] = primal_cot - back
        mixed.append((tau * mix(mix_ref[2 * layer], primal_cot)).astype(BF16).astype(F32))
        extrapolated = (
            2.0 * saved_ref[layer + 1, p].astype(F32) - saved_ref[layer, p].astype(F32)
        ).astype(BF16)
        left.append(jnp.concatenate([extrapolated, *halves(pulled_saved)], 0))
        right.append(jnp.concatenate([*halves(pulled_mixed), *halves(primal_cot)], 0))
    terms = lax.dot_general(
        jnp.concatenate(left, 1),
        jnp.concatenate(right, 1),
        (((1,), (1,)), ((), ())),
        preferred_element_type=F32,
    )
    lane = lax.broadcasted_iota(jnp.int32, (channels, side), 1)
    terms = jnp.where(
        lane < 2 * channels,
        terms[:channels],
        terms[channels : 2 * channels] + terms[2 * channels :],
    )
    terms = terms + pltpu.roll(terms, side - channels, 1)
    half = channels // 2
    packed = jnp.where(
        lax.rem(lane[:half], 2 * channels) < channels,
        terms[:half],
        pltpu.roll(terms[half:], channels, 1),
    ).astype(BF16)

    def one(t):
        at = jnp.broadcast_to(place_ref[t], mixed[0].shape)
        picked = mixed[0]
        for p in range(1, blocks):
            picked = jnp.where(at == p, mixed[p], picked)
        product = lax.dot_general(
            picked.astype(BF16),
            tiles_ref[t],
            (((1,), (1,)), ((), ())),
            preferred_element_type=F32,
        )
        send_ref[t, :channels, :] = product.astype(BF16)
        send_ref[t, channels:, :] = packed

    loop(tiles_ref.shape[0], one)


def per_device(
    tile_blocks,
    tile_rows,
    tile_cols,
    saved_primal,
    saved_dual,
    primal_active,
    dual_active,
    primal_mix,
    dual_mix,
    step_fracs,
    cot_primal,
    cot_dual,
):
    row_count = lax.axis_size("row")
    col_count = lax.axis_size("col")
    owned, channels, side = cot_dual.shape
    primal_count = cot_primal.shape[0]
    layer_count = primal_mix.shape[0]
    row_scale = 1.0 / math.sqrt(owned * row_count * col_count * side)
    col_scale = 1.0 / math.sqrt(primal_count * row_count * side)
    params = pltpu.CompilerParams(vmem_limit_bytes=16 * 1024 * 1024)

    def call(kernel, outs, *operands, ins=None, out_specs=None, **rest):
        return pl.pallas_call(
            kernel,
            out_shape=outs,
            in_specs=ins or [VMEM] * len(operands),
            out_specs=out_specs or jax.tree.map(lambda _: VMEM, outs),
            compiler_params=params,
            **rest,
        )(*operands)

    def exchange(x):
        return lax.all_to_all(x, "row", split_axis=0, concat_axis=0, tiled=True)

    def shape(dims, kind=F32):
        return jax.ShapeDtypeStruct(dims, kind)

    asked = call(
        partial(ask_kernel, owned * col_count, owned),
        shape((row_count, 1, side)),
        pltpu.with_memory_space_constraint(tile_rows, pltpu.HBM),
        ins=[HBM],
        scratch_shapes=[pltpu.SMEM(tile_rows.shape, jnp.int32), pltpu.SemaphoreType.DMA],
    )
    wanted = exchange(asked)
    message = shape((row_count, 2 * channels, side), BF16)
    pushed = shape((row_count, channels + channels // 2, side), BF16)
    terms_shape = shape((channels // 2, side))
    tiles, place, scale, mix, cot, base = call(
        partial(prepare_kernel, owned * col_count, primal_count),
        (
            shape(tile_blocks.shape, BF16),
            shape((row_count, 1, side)),
            shape((2 * layer_count, side)),
            shape((2 * layer_count, channels, side), BF16),
            shape(cot_dual.shape),
            shape((owned, 2 * channels, side), BF16),
        ),
        *(
            pltpu.with_memory_space_constraint(x, pltpu.HBM)
            for x in (
                tile_rows,
                tile_cols,
                step_fracs,
                tile_blocks,
                cot_dual,
                dual_active,
                saved_dual,
                dual_mix,
                primal_mix,
            )
        ),
        ins=[HBM] * 9,
        scratch_shapes=[
            pltpu.VMEM((2 * layer_count, channels, side), F32),
            pltpu.SMEM(tile_rows.shape, jnp.int32),
            pltpu.SMEM(tile_cols.shape, jnp.int32),
            pltpu.SMEM(step_fracs.shape, jnp.int32),
            pltpu.VMEM((owned, side), jnp.int32),
            pltpu.VMEM((owned, channels, side), BF16),
            pltpu.VMEM((2, layer_count, channels, channels), F32),
            pltpu.VMEM(tile_blocks.shape, BF16),
            pltpu.SemaphoreType.DMA((9,)),
        ],
    )
    swap = [(i, col_count - 1 - i) for i in range(col_count)]
    grad_x = cot_primal
    received = None
    all_terms = []
    for layer in reversed(range(layer_count)):
        if received is None:
            send = call(first_dual_kernel, message, wanted, base)
        else:
            cot, send, terms = call(
                partial(dual_kernel, layer),
                (shape(cot_dual.shape), message, terms_shape),
                wanted,
                received,
                cot,
                dual_active,
                saved_dual,
            )
            all_terms.insert(0, terms)
        fetched = exchange(send)
        mine = call(
            pull_kernel, shape((primal_count, 2 * channels, side)), tiles, place, fetched
        )
        other = lax.ppermute(mine, "col", swap)
        grad_x, push = call(
            partial(primal_kernel, layer),
            (shape(cot_primal.shape), pushed),
            tiles,
            place,
            scale,
            mix,
            mine,
            other,
            grad_x,
            primal_active,
            saved_primal,
        )
        received = exchange(push)
    grad_x, grad_y, primal_mix_grad, dual_mix_grad = call(
        partial(last_dual_kernel, row_scale, col_scale),
        (
            shape(cot_primal.shape),
            shape(cot_dual.shape),
            shape(primal_mix.shape),
            shape(dual_mix.shape),
        ),
        wanted,
        received,
        cot,
        scale,
        grad_x,
        *all_terms,
        out_specs=(HBM,) * 4,
        scratch_shapes=[
            pltpu.VMEM(cot_dual.shape, F32),
            pltpu.VMEM(primal_mix.shape, F32),
            pltpu.VMEM(dual_mix.shape, F32),
            pltpu.SemaphoreType.DMA((owned + 3,)),
        ],
    )
    return (grad_x, grad_y, primal_mix_grad, dual_mix_grad)


def solution(mesh):
    return jax.shard_map(
        per_device,
        mesh=mesh,
        in_specs=(
            P(("groups", "row", "col"), None, None),
            P(("groups", "row", "col")),
            P(("groups", "row", "col")),
            P(None, ("groups", "row"), None, None),
            P(None, ("groups", "row", "col"), None, None),
            P(None, ("groups", "row"), None),
            P(None, ("groups", "row", "col"), None),
            P(),
            P(),
            P(),
            P(("groups", "row"), None, None),
            P(("groups", "row", "col"), None, None),
        ),
        out_specs=(
            P(("groups", "row"), None, None),
            P(("groups", "row", "col"), None, None),
            P("groups", None, None),
            P("groups", None, None),
        ),
        check_vma=False,
    )
```

```python
from functools import partial
import math

import jax
import jax.numpy as jnp
from jax import lax
from jax.experimental import pallas as pl
from jax.experimental.pallas import tpu as pltpu
from jax.sharding import PartitionSpec as P

VMEM = pl.BlockSpec(memory_space=pltpu.VMEM)
HBM = pl.BlockSpec(memory_space=pltpu.HBM)
F32 = jnp.float32
BF16 = jnp.bfloat16


def loop(count, body):
    if count <= 16:
        for i in range(count):
            body(i)
    else:
        lax.fori_loop(0, count, lambda i, _: (body(i), 0)[1], 0)


def total_of(count, term, shape):
    if count <= 16:
        total = term(0)
        for i in range(1, count):
            total = total + term(i)
        return total
    return lax.fori_loop(0, count, lambda i, t: t + term(i), jnp.zeros(shape, F32))


def halves(x):
    high = x.astype(BF16)
    return high, (x - high.astype(F32)).astype(BF16)


def slot_of(row, peer_size, shift, row_count):
    return lax.rem(lax.div(row, peer_size) + shift, row_count)


def ask_kernel(slot, owned, rows_in, asked_ref, rows_ref, sem):
    fetch = pltpu.make_async_copy(rows_in, rows_ref, sem)
    fetch.start()
    fetch.wait()

    def one(t):
        place = lax.rem(rows_ref[t], owned)
        filled = jnp.full(asked_ref.shape[1:], place.astype(F32), F32)
        asked_ref[slot(rows_ref[t])] = filled

    loop(asked_ref.shape[0], one)


def prepare_kernel(
    slot,
    primal_count,
    rows_in,
    cols_in,
    steps_in,
    tiles_in,
    cot_in,
    mask_in,
    saved_in,
    dual_mix_in,
    primal_mix_in,
    tiles_ref,
    place_ref,
    scale_ref,
    mix_ref,
    cot_ref,
    base_ref,
    pad_ref,
    rows_ref,
    cols_ref,
    steps_ref,
    mask_ref,
    saved_ref,
    mixes_ref,
    held_ref,
    sems,
):
    owned, channels, side = cot_ref.shape
    layers = dual_mix_in.shape[0]
    fetches = [
        pltpu.make_async_copy(source, target, sems.at[i])
        for i, (source, target) in enumerate(
            (
                (rows_in, rows_ref),
                (cols_in, cols_ref),
                (steps_in, steps_ref),
                (tiles_in, held_ref),
                (cot_in, cot_ref),
                (saved_in.at[layers - 1], saved_ref),
                (mask_in.at[layers - 1], mask_ref),
                (primal_mix_in, mixes_ref.at[0]),
                (dual_mix_in, mixes_ref.at[1]),
            )
        )
    ]
    for fetch in fetches:
        fetch.start()
    pad_ref[...] = jnp.zeros_like(pad_ref)
    for fetch in fetches[:3]:
        fetch.wait()

    def one(t):
        p = lax.rem(cols_ref[t], primal_count)
        filled = jnp.full(place_ref.shape[1:], p.astype(F32), F32)
        place_ref[slot(rows_ref[t])] = filled

    loop(tiles_ref.shape[0], one)
    for k in range(layers):
        for s in range(2):
            upper = jnp.full((1, side), steps_ref[k, 2 * s].astype(F32), F32)
            lower = jnp.full((1, side), steps_ref[k, 2 * s + 1].astype(F32), F32)
            scale_ref[pl.ds(2 * k + s, 1), :] = -(upper / lower)
    for fetch in fetches[7:]:
        fetch.wait()
    for k in range(layers):
        for s in range(2):
            pad_ref[2 * k + s, :, :channels] = mixes_ref[s, k]
            weights = pad_ref[2 * k + s]
            high = weights.astype(BF16).astype(F32)
            rest = weights - high
            mix_ref[2 * k + s] = (
                high
                + pltpu.roll(high, channels, 1)
                + pltpu.roll(rest, 2 * channels, 1)
                + pltpu.roll(rest, 3 * channels, 1)
            ).astype(BF16)
    for fetch in fetches[4:7]:
        fetch.wait()
    for b in range(owned):
        cot = mask_ref[pl.ds(b, 1), :].astype(F32) * cot_ref[b]
        cot_ref[b] = cot
        base_ref[b, :channels, :] = cot.astype(BF16)
        base_ref[b, channels:, :] = saved_ref[b]
    fetches[3].wait()

    def sort(t):
        tiles_ref[slot(rows_ref[t])] = held_ref[t]

    loop(tiles_ref.shape[0], sort)


def choose(place_ref, base, send_ref):
    def one(r):
        place = jnp.broadcast_to(place_ref[r], base[0].shape)
        picked = base[0]
        for b in range(1, len(base)):
            picked = jnp.where(place == b, base[b], picked)
        send_ref[r] = picked.astype(BF16)

    loop(send_ref.shape[0], one)


def first_dual_kernel(wanted_ref, base_ref, send_ref):
    owned = base_ref.shape[0]
    choose(wanted_ref, [base_ref[b].astype(F32) for b in range(owned)], send_ref)


def add_pushed(wanted_ref, received_ref, cot_ref):
    owned, channels, side = cot_ref.shape
    rows = received_ref.shape[0]
    place = lambda r: jnp.broadcast_to(wanted_ref[r], (channels, side))
    if rows <= 16:
        blocks = [cot_ref[b] for b in range(owned)]
        for r in range(rows):
            at, pushed = place(r), received_ref[r, :channels, :].astype(F32)
            blocks = [block + jnp.where(at == b, pushed, 0.0) for b, block in enumerate(blocks)]
        return blocks

    def step(r, blocks):
        at, pushed = place(r), received_ref[r, :channels, :].astype(F32)
        return tuple(block + jnp.where(at == b, pushed, 0.0) for b, block in enumerate(blocks))

    return list(lax.fori_loop(0, rows, step, tuple(cot_ref[b] for b in range(owned))))


def sum_terms(received_ref, channels):
    rows, height, side = received_ref.shape
    return total_of(
        rows, lambda r: received_ref[r, channels:, :].astype(F32), (height - channels, side)
    )


def dual_kernel(
    layer, wanted_ref, received_ref, cot_in, mask_ref, saved_ref, cot_ref, send_ref, terms_ref
):
    base = []
    for b, block in enumerate(add_pushed(wanted_ref, received_ref, cot_in)):
        cot = mask_ref[layer, pl.ds(b, 1), :].astype(F32) * block
        cot_ref[b] = cot
        base.append(jnp.concatenate([cot, saved_ref[layer, b].astype(F32)], 0))
    choose(wanted_ref, base, send_ref)
    terms_ref[...] = sum_terms(received_ref, cot_ref.shape[1])


def last_dual_kernel(
    row_scale, col_scale, wanted_ref, received_ref, cot_in, scale_ref, grad_in, *refs
):
    terms_refs, refs = refs[:-8], refs[-8:]
    grad_ref, cot_ref, primal_out, dual_out, held_ref, primal_ref, dual_ref, sems = refs
    owned, channels, side = held_ref.shape
    layers = primal_ref.shape[0]
    copies = [pltpu.make_async_copy(grad_in, grad_ref, sems.at[owned])]
    copies[0].start()
    for b, block in enumerate(add_pushed(wanted_ref, received_ref, cot_in)):
        held_ref[b] = block
        copy = pltpu.make_async_copy(held_ref.at[b], cot_ref.at[b], sems.at[b])
        copy.start()
        copies.append(copy)
    for k in range(layers):
        terms = sum_terms(received_ref, channels) if k == 0 else terms_refs[k - 1][...]
        half = terms.shape[0]
        dual = scale_ref[pl.ds(2 * k + 1, 1), :] * row_scale * terms
        primal = scale_ref[pl.ds(2 * k, 1), :] * col_scale * terms
        dual_ref[k, :half, :] = dual[:, :channels]
        dual_ref[k, half:, :] = pltpu.roll(dual, side - channels, 1)[:, :channels]
        primal_ref[k, :half, :] = pltpu.roll(primal, side - 2 * channels, 1)[:, :channels]
        primal_ref[k, half:, :] = pltpu.roll(primal, side - 3 * channels, 1)[:, :channels]
    for i, (source, target) in enumerate(((primal_ref, primal_out), (dual_ref, dual_out))):
        copies.append(pltpu.make_async_copy(source, target, sems.at[owned + 1 + i]))
        copies[-1].start()
    for copy in copies:
        copy.wait()


def pull_kernel(tiles_ref, place_ref, received_ref, sum_ref):
    count = sum_ref.shape[0]
    rows = tiles_ref.shape[0]

    def step(t, sums):
        product = jnp.dot(received_ref[t], tiles_ref[t], preferred_element_type=F32)
        at = jnp.broadcast_to(place_ref[t], product.shape)
        return tuple(s + jnp.where(at == p, product, 0.0) for p, s in enumerate(sums))

    sums = tuple(jnp.zeros(sum_ref.shape[1:], F32) for _ in range(count))
    if rows <= 16:
        for t in range(rows):
            sums = step(t, sums)
    else:
        sums = lax.fori_loop(0, rows, step, sums)
    for p in range(count):
        sum_ref[p] = sums[p]


def primal_kernel(
    layer,
    tiles_ref,
    place_ref,
    scale_ref,
    mix_ref,
    mine_ref,
    other_ref,
    grad_in,
    mask_ref,
    saved_ref,
    grad_ref,
    send_ref,
):
    blocks, channels, side = grad_ref.shape
    sigma = scale_ref[pl.ds(2 * layer + 1, 1), :]
    tau = scale_ref[pl.ds(2 * layer, 1), :]

    def mix(weights, x):
        high, rest = halves(x)
        return jnp.dot(
            weights, jnp.concatenate([high, rest, high, rest], 0), preferred_element_type=F32
        )

    mixed, left, right = [], [], []
    for p in range(blocks):
        both = mine_ref[p] + other_ref[p]
        pulled_mixed, pulled_saved = both[:channels], both[channels:]
        back = sigma * mix(mix_ref[2 * layer + 1], pulled_mixed)
        primal_cot = mask_ref[layer, pl.ds(p, 1), :].astype(F32) * (grad_in[p] + 2.0 * back)
        grad_ref[p] = primal_cot - back
        mixed.append((tau * mix(mix_ref[2 * layer], primal_cot)).astype(BF16).astype(F32))
        extrapolated = (
            2.0 * saved_ref[layer + 1, p].astype(F32) - saved_ref[layer, p].astype(F32)
        ).astype(BF16)
        left.append(jnp.concatenate([extrapolated, *halves(pulled_saved)], 0))
        right.append(jnp.concatenate([*halves(pulled_mixed), *halves(primal_cot)], 0))
    terms = lax.dot_general(
        jnp.concatenate(left, 1),
        jnp.concatenate(right, 1),
        (((1,), (1,)), ((), ())),
        preferred_element_type=F32,
    )
    lane = lax.broadcasted_iota(jnp.int32, (channels, side), 1)
    terms = jnp.where(
        lane < 2 * channels,
        terms[:channels],
        terms[channels : 2 * channels] + terms[2 * channels :],
    )
    terms = terms + pltpu.roll(terms, side - channels, 1)
    half = channels // 2
    packed = jnp.where(
        lax.rem(lane[:half], 2 * channels) < channels,
        terms[:half],
        pltpu.roll(terms[half:], channels, 1),
    ).astype(BF16)

    def one(t):
        at = jnp.broadcast_to(place_ref[t], mixed[0].shape)
        picked = mixed[0]
        for p in range(1, blocks):
            picked = jnp.where(at == p, mixed[p], picked)
        product = lax.dot_general(
            picked.astype(BF16),
            tiles_ref[t],
            (((1,), (1,)), ((), ())),
            preferred_element_type=F32,
        )
        send_ref[t, :channels, :] = product.astype(BF16)
        send_ref[t, channels:, :] = packed

    loop(tiles_ref.shape[0], one)


def per_device(
    tile_blocks,
    tile_rows,
    tile_cols,
    saved_primal,
    saved_dual,
    primal_active,
    dual_active,
    primal_mix,
    dual_mix,
    step_fracs,
    cot_primal,
    cot_dual,
):
    row_count = lax.axis_size("row")
    col_count = lax.axis_size("col")
    owned, channels, side = cot_dual.shape
    primal_count = cot_primal.shape[0]
    layer_count = primal_mix.shape[0]
    row_scale = 1.0 / math.sqrt(owned * row_count * col_count * side)
    col_scale = 1.0 / math.sqrt(primal_count * row_count * side)
    params = pltpu.CompilerParams(vmem_limit_bytes=16 * 1024 * 1024)

    def call(kernel, outs, *operands, ins=None, out_specs=None, **rest):
        return pl.pallas_call(
            kernel,
            out_shape=outs,
            in_specs=ins or [VMEM] * len(operands),
            out_specs=out_specs or jax.tree.map(lambda _: VMEM, outs),
            compiler_params=params,
            **rest,
        )(*operands)

    shift = row_count - row_count // 2
    order = [(slot + row_count - shift) % row_count for slot in range(row_count)]

    def exchange(x):
        return lax.all_to_all(
            x, "row", split_axis=0, concat_axis=0, axis_index_groups=[order], tiled=True
        )

    def shape(dims, kind=F32):
        return jax.ShapeDtypeStruct(dims, kind)

    slot = partial(slot_of, peer_size=owned * col_count, shift=shift, row_count=row_count)
    asked = call(
        partial(ask_kernel, slot, owned),
        shape((row_count, 1, side)),
        pltpu.with_memory_space_constraint(tile_rows, pltpu.HBM),
        ins=[HBM],
        scratch_shapes=[pltpu.SMEM(tile_rows.shape, jnp.int32), pltpu.SemaphoreType.DMA],
    )
    wanted = exchange(asked)
    message = shape((row_count, 2 * channels, side), BF16)
    pushed = shape((row_count, channels + channels // 2, side), BF16)
    terms_shape = shape((channels // 2, side))
    tiles, place, scale, mix, cot, base = call(
        partial(prepare_kernel, slot, primal_count),
        (
            shape(tile_blocks.shape, BF16),
            shape((row_count, 1, side)),
            shape((2 * layer_count, side)),
            shape((2 * layer_count, channels, side), BF16),
            shape(cot_dual.shape),
            shape((owned, 2 * channels, side), BF16),
        ),
        *(
            pltpu.with_memory_space_constraint(x, pltpu.HBM)
            for x in (
                tile_rows,
                tile_cols,
                step_fracs,
                tile_blocks,
                cot_dual,
                dual_active,
                saved_dual,
                dual_mix,
                primal_mix,
            )
        ),
        ins=[HBM] * 9,
        scratch_shapes=[
            pltpu.VMEM((2 * layer_count, channels, side), F32),
            pltpu.SMEM(tile_rows.shape, jnp.int32),
            pltpu.SMEM(tile_cols.shape, jnp.int32),
            pltpu.SMEM(step_fracs.shape, jnp.int32),
            pltpu.VMEM((owned, side), jnp.int32),
            pltpu.VMEM((owned, channels, side), BF16),
            pltpu.VMEM((2, layer_count, channels, channels), F32),
            pltpu.VMEM(tile_blocks.shape, BF16),
            pltpu.SemaphoreType.DMA((9,)),
        ],
    )
    swap = [(i, col_count - 1 - i) for i in range(col_count)]
    grad_x = cot_primal
    received = None
    all_terms = []
    for layer in reversed(range(layer_count)):
        if received is None:
            send = call(first_dual_kernel, message, wanted, base)
        else:
            cot, send, terms = call(
                partial(dual_kernel, layer),
                (shape(cot_dual.shape), message, terms_shape),
                wanted,
                received,
                cot,
                dual_active,
                saved_dual,
            )
            all_terms.insert(0, terms)
        fetched = exchange(send)
        mine = call(
            pull_kernel, shape((primal_count, 2 * channels, side)), tiles, place, fetched
        )
        other = lax.ppermute(mine, "col", swap)
        grad_x, push = call(
            partial(primal_kernel, layer),
            (shape(cot_primal.shape), pushed),
            tiles,
            place,
            scale,
            mix,
            mine,
            other,
            grad_x,
            primal_active,
            saved_primal,
        )
        received = exchange(push)
    grad_x, grad_y, primal_mix_grad, dual_mix_grad = call(
        partial(last_dual_kernel, row_scale, col_scale),
        (
            shape(cot_primal.shape),
            shape(cot_dual.shape),
            shape(primal_mix.shape),
            shape(dual_mix.shape),
        ),
        wanted,
        received,
        cot,
        scale,
        grad_x,
        *all_terms,
        out_specs=(HBM,) * 4,
        scratch_shapes=[
            pltpu.VMEM(cot_dual.shape, F32),
            pltpu.VMEM(primal_mix.shape, F32),
            pltpu.VMEM(dual_mix.shape, F32),
            pltpu.SemaphoreType.DMA((owned + 3,)),
        ],
    )
    return (grad_x, grad_y, primal_mix_grad, dual_mix_grad)


def solution(mesh):
    return jax.shard_map(
        per_device,
        mesh=mesh,
        in_specs=(
            P(("groups", "row", "col"), None, None),
            P(("groups", "row", "col")),
            P(("groups", "row", "col")),
            P(None, ("groups", "row"), None, None),
            P(None, ("groups", "row", "col"), None, None),
            P(None, ("groups", "row"), None),
            P(None, ("groups", "row", "col"), None),
            P(),
            P(),
            P(),
            P(("groups", "row"), None, None),
            P(("groups", "row", "col"), None, None),
        ),
        out_specs=(
            P(("groups", "row"), None, None),
            P(("groups", "row", "col"), None, None),
            P("groups", None, None),
            P("groups", None, None),
        ),
        check_vma=False,
    )
```

```python
from functools import partial
import math

import jax
import jax.numpy as jnp
from jax import lax
from jax.experimental import pallas as pl
from jax.experimental.pallas import tpu as pltpu
from jax.sharding import PartitionSpec as P

VMEM = pl.BlockSpec(memory_space=pltpu.VMEM)
HBM = pl.BlockSpec(memory_space=pltpu.HBM)
F32 = jnp.float32
BF16 = jnp.bfloat16


def loop(count, body):
    if count <= 16:
        for i in range(count):
            body(i)
    else:
        lax.fori_loop(0, count, lambda i, _: (body(i), 0)[1], 0)


def total_of(count, term, shape):
    if count <= 16:
        total = term(0)
        for i in range(1, count):
            total = total + term(i)
        return total
    return lax.fori_loop(0, count, lambda i, t: t + term(i), jnp.zeros(shape, F32))


def halves(x):
    high = x.astype(BF16)
    return high, (x - high.astype(F32)).astype(BF16)


def slot_of(row, peer_size, shift, row_count):
    return lax.rem(lax.div(row, peer_size) + shift, row_count)


def ask_kernel(slot, owned, rows_in, asked_ref, rows_ref, sem):
    fetch = pltpu.make_async_copy(rows_in, rows_ref, sem)
    fetch.start()
    fetch.wait()

    def one(t):
        place = lax.rem(rows_ref[t], owned)
        filled = jnp.full(asked_ref.shape[1:], place.astype(F32), F32)
        asked_ref[slot(rows_ref[t])] = filled

    loop(asked_ref.shape[0], one)


def prepare_kernel(
    slot,
    primal_count,
    rows_in,
    cols_in,
    steps_in,
    tiles_in,
    cot_in,
    mask_in,
    dual_mix_in,
    primal_mix_in,
    tiles_ref,
    scale_ref,
    mix_ref,
    cot_ref,
    pad_ref,
    rows_ref,
    cols_ref,
    steps_ref,
    mask_ref,
    mixes_ref,
    held_ref,
    sems,
):
    owned, channels, side = cot_ref.shape
    layers = dual_mix_in.shape[0]
    fetches = [
        pltpu.make_async_copy(source, target, sems.at[i])
        for i, (source, target) in enumerate(
            (
                (rows_in, rows_ref),
                (cols_in, cols_ref),
                (steps_in, steps_ref),
                (tiles_in, held_ref),
                (cot_in, cot_ref),
                (mask_in.at[layers - 1], mask_ref),
                (primal_mix_in, mixes_ref.at[0]),
                (dual_mix_in, mixes_ref.at[1]),
            )
        )
    ]
    for fetch in fetches:
        fetch.start()
    pad_ref[...] = jnp.zeros_like(pad_ref)
    for fetch in fetches[:3]:
        fetch.wait()
    for k in range(layers):
        for s in range(2):
            upper = jnp.full((1, side), steps_ref[k, 2 * s].astype(F32), F32)
            lower = jnp.full((1, side), steps_ref[k, 2 * s + 1].astype(F32), F32)
            scale_ref[pl.ds(2 * k + s, 1), :] = -(upper / lower)
    for fetch in fetches[6:]:
        fetch.wait()
    for k in range(layers):
        for s in range(2):
            pad_ref[2 * k + s, :, :channels] = mixes_ref[s, k]
            weights = pad_ref[2 * k + s]
            high = weights.astype(BF16).astype(F32)
            rest = weights - high
            mix_ref[2 * k + s] = (
                high
                + pltpu.roll(high, channels, 1)
                + pltpu.roll(rest, 2 * channels, 1)
                + pltpu.roll(rest, 3 * channels, 1)
            ).astype(BF16)
    for fetch in fetches[4:6]:
        fetch.wait()
    for b in range(owned):
        cot_ref[b] = mask_ref[pl.ds(b, 1), :].astype(F32) * cot_ref[b]
    fetches[3].wait()
    below = tiles_ref.shape[1] - held_ref.shape[1]

    def sort(t):
        to = slot(rows_ref[t])
        tiles_ref[to, : held_ref.shape[1], :] = held_ref[t]
        p = lax.rem(cols_ref[t], primal_count)
        filled = jnp.full((below, side), p.astype(F32), F32)
        tiles_ref[to, held_ref.shape[1] :, :] = filled.astype(BF16)

    loop(tiles_ref.shape[0], sort)


def chosen(wanted_ref, r, base):
    place = jnp.broadcast_to(wanted_ref[r], base[0].shape)
    picked = base[0]
    for b in range(1, len(base)):
        picked = jnp.where(place == b, base[b], picked)
    return picked.astype(BF16)


def choose_for_all(wanted_ref, base, send_ref):
    cols = send_ref.shape[0] // wanted_ref.shape[0]

    def one(r):
        picked = chosen(wanted_ref, r, base)
        for c in range(cols):
            send_ref[r * cols + c] = picked

    loop(wanted_ref.shape[0], one)


def first_dual_kernel(wanted_ref, cot_ref, send_ref):
    choose_for_all(wanted_ref, [cot_ref[b] for b in range(cot_ref.shape[0])], send_ref)


def sum_pushed(wanted_ref, received_ref, start):
    channels, side = start[0].shape
    rows = received_ref.shape[0]

    def step(r, blocks):
        at = jnp.broadcast_to(wanted_ref[r], (channels, side))
        pushed = received_ref[r, :channels, :].astype(F32)
        return tuple(block + jnp.where(at == b, pushed, 0.0) for b, block in enumerate(blocks))

    blocks = tuple(start)
    if rows <= 16:
        for r in range(rows):
            blocks = step(r, blocks)
        return blocks
    return lax.fori_loop(0, rows, step, blocks)


def place_of(tiles_ref, t, shape):
    side = tiles_ref.shape[2]
    return jnp.broadcast_to(tiles_ref[t, side:, :].astype(F32)[:1], shape)


def mixed_by(weights, blocks):
    side = blocks[0].shape[1]
    high, rest = halves(jnp.concatenate(blocks, 1))
    mixed = jnp.dot(
        weights, jnp.concatenate([high, rest, high, rest], 0), preferred_element_type=F32
    )
    return [mixed[:, b * side : (b + 1) * side] for b in range(len(blocks))]


def folded(terms, channels):
    return terms + pltpu.roll(terms, terms.shape[1] - channels, 1)


def contract(left, right):
    return lax.dot_general(
        jnp.concatenate(left, 1),
        jnp.concatenate(right, 1),
        (((1,), (1,)), ((), ())),
        preferred_element_type=F32,
    )


def dual_kernel(
    layer,
    wanted_ref,
    received_ref,
    cot_in,
    mask_ref,
    saved_ref,
    scale_ref,
    mix_ref,
    *refs,
):
    owned, channels, side = cot_in.shape
    tiles_refs, (cot_ref, send_ref, terms_ref) = refs[:-3], refs[-3:]
    above = layer + 1
    tau = scale_ref[pl.ds(2 * above, 1), :]
    pushed = sum_pushed(
        wanted_ref, received_ref, [jnp.zeros((channels, side), F32) for _ in range(owned)]
    )
    base, left, right = [], [], []
    mixed = mixed_by(mix_ref[2 * above], pushed)
    for b in range(owned):
        block = cot_in[b] + tau * mixed[b]
        cot = mask_ref[layer, pl.ds(b, 1), :].astype(F32) * block
        cot_ref[b] = cot
        base.append(cot)
        high, rest = halves(pushed[b])
        left.append(saved_ref[above, b])
        right.append(jnp.concatenate([high, rest, high, rest], 0))
    choose_for_all(wanted_ref, base, send_ref)
    terms_ref[0] = folded(contract(left, right), channels)
    for tiles_ref in tiles_refs:
        count = terms_ref.shape[0] - 1

        def step(t, sums):
            product = jnp.dot(
                received_ref[t, channels:, :], tiles_ref[t, :side, :], preferred_element_type=F32
            )
            at = place_of(tiles_ref, t, product.shape)
            return tuple(s + jnp.where(at == p, product, 0.0) for p, s in enumerate(sums))

        sums = tuple(jnp.zeros((channels, side), F32) for _ in range(count))
        if received_ref.shape[0] <= 16:
            for t in range(received_ref.shape[0]):
                sums = step(t, sums)
        else:
            sums = lax.fori_loop(0, received_ref.shape[0], step, sums)
        for p in range(count):
            terms_ref[1 + p] = sums[p]


def last_dual_kernel(
    row_scale,
    col_scale,
    wanted_ref,
    received_ref,
    cot_in,
    scale_ref,
    grad_in,
    grad_ref,
    cot_ref,
    primal_out,
    dual_out,
    held_ref,
    primal_ref,
    dual_ref,
    sems,
):
    owned, channels, side = held_ref.shape
    layers = primal_ref.shape[0]
    half = channels // 2
    rows = received_ref.shape[0]
    copies = [pltpu.make_async_copy(grad_in, grad_ref, sems.at[owned])]
    copies[0].start()
    blocks = sum_pushed(wanted_ref, received_ref, [cot_in[b] for b in range(owned)])
    for b, block in enumerate(blocks):
        held_ref[b] = block
        copy = pltpu.make_async_copy(held_ref.at[b], cot_ref.at[b], sems.at[b])
        copy.start()
        copies.append(copy)
    all_terms = total_of(
        rows, lambda r: received_ref[r, channels:, :].astype(F32), (layers * half, side)
    )
    for k in range(layers):
        terms = all_terms[k * half : (k + 1) * half]
        dual = scale_ref[pl.ds(2 * k + 1, 1), :] * row_scale * terms
        primal = scale_ref[pl.ds(2 * k, 1), :] * col_scale * terms
        dual_ref[k, :half, :] = dual[:, :channels]
        dual_ref[k, half:, :] = pltpu.roll(dual, side - channels, 1)[:, :channels]
        primal_ref[k, :half, :] = pltpu.roll(primal, side - 2 * channels, 1)[:, :channels]
        primal_ref[k, half:, :] = pltpu.roll(primal, side - 3 * channels, 1)[:, :channels]
    for i, (source, target) in enumerate(((primal_ref, primal_out), (dual_ref, dual_out))):
        copies.append(pltpu.make_async_copy(source, target, sems.at[owned + 1 + i]))
        copies[-1].start()
    for copy in copies:
        copy.wait()


def primal_step(layer, shared, grad_ref):
    tiles_ref, other_ref, scale_ref, mix_ref, fetched_ref, grad_in, mask_ref, saved_ref = shared
    blocks, channels, side = grad_ref.shape
    rows = tiles_ref.shape[0]
    me = lax.axis_index("col")
    sigma = scale_ref[pl.ds(2 * layer + 1, 1), :]

    def step(t, sums):
        for tiles, message in ((tiles_ref, 2 * t + 1 - me), (other_ref, 2 * t + me)):
            product = jnp.dot(
                fetched_ref[message], tiles[t, :side, :], preferred_element_type=F32
            )
            at = place_of(tiles, t, product.shape)
            sums = tuple(s + jnp.where(at == p, product, 0.0) for p, s in enumerate(sums))
        return sums

    sums = tuple(jnp.zeros((channels, side), F32) for _ in range(blocks))
    if rows <= 16:
        for t in range(rows):
            sums = step(t, sums)
    else:
        sums = lax.fori_loop(0, rows, step, sums)
    cots, extrapolated = [], []
    mixed = mixed_by(mix_ref[2 * layer + 1], sums)
    for p in range(blocks):
        back = sigma * mixed[p]
        cot = mask_ref[layer, pl.ds(p, 1), :].astype(F32) * (grad_in[p] + 2.0 * back)
        grad_ref[p] = cot - back
        cots.append(cot)
        extrapolated.append(
            (
                2.0 * saved_ref[layer + 1, p].astype(F32) - saved_ref[layer, p].astype(F32)
            ).astype(BF16)
        )
    return sums, cots, extrapolated


def push(tiles_ref, blocks, send_ref, below):
    channels, side = blocks[0].shape

    def one(t):
        at = place_of(tiles_ref, t, blocks[0].shape)
        picked = blocks[0]
        for p in range(1, len(blocks)):
            picked = jnp.where(at == p, blocks[p], picked)
        product = lax.dot_general(
            picked.astype(BF16),
            tiles_ref[t, :side, :],
            (((1,), (1,)), ((), ())),
            preferred_element_type=F32,
        )
        send_ref[t, :channels, :] = product.astype(BF16)
        if below is not None:
            send_ref[t, channels:, :] = below(t)

    loop(tiles_ref.shape[0], one)


def primal_kernel(layer, *refs):
    shared, rest, (grad_ref, send_ref, terms_ref) = refs[:8], refs[8:-3], refs[-3:]
    blocks, channels, side = grad_ref.shape
    sums, cots, extrapolated = primal_step(layer, shared, grad_ref)
    below = None
    if rest:
        wanted_ref, dual_ref = rest
        base = [dual_ref[0, b].astype(F32) for b in range(dual_ref.shape[1])]
        below = lambda t: chosen(wanted_ref, t, base)
    push(shared[0], cots, send_ref, below)
    right = []
    for p in range(blocks):
        high, low = halves(sums[p])
        right.append(jnp.concatenate([high, low, high, low], 0))
    terms_ref[...] = folded(contract(extrapolated, right), channels)


def last_primal_kernel(*refs):
    shared, rest, (grad_ref, send_ref) = refs[:8], refs[8:-2], refs[-2:]
    early_ref, early_other, late_ref, late_other, *dual_terms = rest
    scale_ref, mix_ref = shared[2], shared[3]
    blocks, channels, side = grad_ref.shape
    half = channels // 2
    sums, cots, extrapolated = primal_step(0, shared, grad_ref)
    tau = scale_ref[pl.ds(0, 1), :]
    left, right = [], []
    for p in range(blocks):
        pulled = early_ref[1 + p] + early_other[1 + p]
        left.append(jnp.concatenate([extrapolated[p], *halves(pulled)], 0))
        right.append(jnp.concatenate([*halves(sums[p]), *halves(cots[p])], 0))
    terms = contract(left, right)
    lane = lax.broadcasted_iota(jnp.int32, (channels, side), 1)
    low = lane < 2 * channels
    terms = jnp.where(
        low, terms[:channels], terms[channels : 2 * channels] + terms[2 * channels :]
    )
    primal_terms = (late_ref[0] + late_other[0], early_ref[0] + early_other[0])
    all_terms = [folded(terms, channels)] + [
        jnp.where(low, dual[...], primal) for dual, primal in zip(dual_terms, primal_terms)
    ]
    packed = jnp.concatenate(
        [
            jnp.where(
                lax.rem(lane[:half], 2 * channels) < channels,
                one[:half],
                pltpu.roll(one[half:], channels, 1),
            )
            for one in all_terms
        ],
        0,
    ).astype(BF16)
    mixed = [
        (tau * cot).astype(BF16).astype(F32) for cot in mixed_by(mix_ref[0], cots)
    ]
    push(shared[0], mixed, send_ref, lambda t: packed)


def per_device(
    tile_blocks,
    tile_rows,
    tile_cols,
    saved_primal,
    saved_dual,
    primal_active,
    dual_active,
    primal_mix,
    dual_mix,
    step_fracs,
    cot_primal,
    cot_dual,
):
    row_count = lax.axis_size("row")
    col_count = lax.axis_size("col")
    owned, channels, side = cot_dual.shape
    primal_count = cot_primal.shape[0]
    layer_count = primal_mix.shape[0]
    half = channels // 2
    row_scale = 1.0 / math.sqrt(owned * row_count * col_count * side)
    col_scale = 1.0 / math.sqrt(primal_count * row_count * side)
    params = pltpu.CompilerParams(vmem_limit_bytes=24 * 1024 * 1024)

    def call(kernel, outs, *operands, ins=None, out_specs=None, **rest):
        return pl.pallas_call(
            kernel,
            out_shape=outs,
            in_specs=ins or [VMEM] * len(operands),
            out_specs=out_specs or jax.tree.map(lambda _: VMEM, outs),
            compiler_params=params,
            **rest,
        )(*operands)

    shift = row_count - row_count // 2
    order = [(slot + row_count - shift) % row_count for slot in range(row_count)]
    order_all = [row * col_count + c for row in order for c in reversed(range(col_count))]

    def exchange(x, axes="row", group=order):
        return lax.all_to_all(
            x, axes, split_axis=0, concat_axis=0, axis_index_groups=[group], tiled=True
        )

    def shape(dims, kind=F32):
        return jax.ShapeDtypeStruct(dims, kind)

    def in_hbm(*arrays):
        return [pltpu.with_memory_space_constraint(x, pltpu.HBM) for x in arrays]

    def swap(x):
        return lax.ppermute(x, "col", [(i, col_count - 1 - i) for i in range(col_count)])

    slot = partial(slot_of, peer_size=owned * col_count, shift=shift, row_count=row_count)
    asked = call(
        partial(ask_kernel, slot, owned),
        shape((row_count, 1, side)),
        *in_hbm(tile_rows),
        ins=[HBM],
        scratch_shapes=[pltpu.SMEM(tile_rows.shape, jnp.int32), pltpu.SemaphoreType.DMA],
    )
    wanted = exchange(asked)
    tiles, scale, mix, cot = call(
        partial(prepare_kernel, slot, primal_count),
        (
            shape((row_count, side + 16, side), BF16),
            shape((2 * layer_count, side)),
            shape((2 * layer_count, channels, side), BF16),
            shape(cot_dual.shape),
        ),
        *in_hbm(
            tile_rows,
            tile_cols,
            step_fracs,
            tile_blocks,
            cot_dual,
            dual_active,
            dual_mix,
            primal_mix,
        ),
        ins=[HBM] * 8,
        scratch_shapes=[
            pltpu.VMEM((2 * layer_count, channels, side), F32),
            pltpu.SMEM(tile_rows.shape, jnp.int32),
            pltpu.SMEM(tile_cols.shape, jnp.int32),
            pltpu.SMEM(step_fracs.shape, jnp.int32),
            pltpu.VMEM((owned, side), jnp.int32),
            pltpu.VMEM((2, layer_count, channels, channels), F32),
            pltpu.VMEM(tile_blocks.shape, BF16),
            pltpu.SemaphoreType.DMA((8,)),
        ],
    )
    other_tiles = swap(lax.optimization_barrier((tiles, wanted))[0])
    blocks_out = shape((col_count * row_count, channels, side), BF16)
    grad_x = cot_primal
    send = call(first_dual_kernel, blocks_out, wanted, cot)
    dual_terms, primal_terms = [], []
    for layer in reversed(range(layer_count)):
        fetched = exchange(send, ("row", "col"), order_all)
        shared = (
            tiles,
            other_tiles,
            scale,
            mix,
            fetched,
            grad_x,
            primal_active,
            saved_primal,
        )
        if layer == 0:
            height = channels + layer_count * half
            grad_x, pushed = call(
                last_primal_kernel,
                (shape(cot_primal.shape), shape((row_count, height, side), BF16)),
                *shared,
                *primal_terms,
                *dual_terms[::-1],
            )
            received = exchange(pushed)
            break
        first = layer == layer_count - 1
        height = 2 * channels if first else channels
        grad_x, pushed, terms = call(
            partial(primal_kernel, layer),
            (
                shape(cot_primal.shape),
                shape((row_count, height, side), BF16),
                shape((channels, side)),
            ),
            *shared,
            *((wanted, saved_dual) if first else ()),
        )
        dual_terms.append(terms)
        received = exchange(pushed)
        cot, send, terms = call(
            partial(dual_kernel, layer - 1),
            (
                shape(cot_dual.shape),
                blocks_out,
                shape((1 + (primal_count if first else 0), channels, side)),
            ),
            wanted,
            received,
            cot,
            dual_active,
            saved_dual,
            scale,
            mix,
            *((tiles,) if first else ()),
        )
        primal_terms += [terms, swap(terms)]
    grad_x, grad_y, primal_mix_grad, dual_mix_grad = call(
        partial(last_dual_kernel, row_scale, col_scale),
        (
            shape(cot_primal.shape),
            shape(cot_dual.shape),
            shape(primal_mix.shape),
            shape(dual_mix.shape),
        ),
        wanted,
        received,
        cot,
        scale,
        grad_x,
        out_specs=(HBM,) * 4,
        scratch_shapes=[
            pltpu.VMEM(cot_dual.shape, F32),
            pltpu.VMEM(primal_mix.shape, F32),
            pltpu.VMEM(dual_mix.shape, F32),
            pltpu.SemaphoreType.DMA((owned + 3,)),
        ],
    )
    return (grad_x, grad_y, primal_mix_grad, dual_mix_grad)


def solution(mesh):
    return jax.shard_map(
        per_device,
        mesh=mesh,
        in_specs=(
            P(("groups", "row", "col"), None, None),
            P(("groups", "row", "col")),
            P(("groups", "row", "col")),
            P(None, ("groups", "row"), None, None),
            P(None, ("groups", "row", "col"), None, None),
            P(None, ("groups", "row"), None),
            P(None, ("groups", "row", "col"), None),
            P(),
            P(),
            P(),
            P(("groups", "row"), None, None),
            P(("groups", "row", "col"), None, None),
        ),
        out_specs=(
            P(("groups", "row"), None, None),
            P(("groups", "row", "col"), None, None),
            P("groups", None, None),
            P("groups", None, None),
        ),
        check_vma=False,
    )
```

```python
from functools import partial
import math

import jax
import jax.numpy as jnp
from jax import lax
from jax.experimental import pallas as pl
from jax.experimental.pallas import tpu as pltpu
from jax.sharding import PartitionSpec as P

VMEM = pl.BlockSpec(memory_space=pltpu.VMEM)
HBM = pl.BlockSpec(memory_space=pltpu.HBM)
F32 = jnp.float32
BF16 = jnp.bfloat16


def loop(count, body):
    if count <= 16:
        for i in range(count):
            body(i)
    else:
        lax.fori_loop(0, count, lambda i, _: (body(i), 0)[1], 0)


def total_of(count, term, shape):
    if count <= 16:
        total = term(0)
        for i in range(1, count):
            total = total + term(i)
        return total
    return lax.fori_loop(0, count, lambda i, t: t + term(i), jnp.zeros(shape, F32))


def halves(x):
    high = x.astype(BF16)
    return high, (x - high.astype(F32)).astype(BF16)


def slot_of(row, peer_size, shift, row_count):
    return lax.rem(lax.div(row, peer_size) + shift, row_count)


def ask_kernel(slot, owned, rows_in, asked_ref, rows_ref, sem):
    fetch = pltpu.make_async_copy(rows_in, rows_ref, sem)
    fetch.start()
    fetch.wait()

    def one(t):
        place = lax.rem(rows_ref[t], owned)
        filled = jnp.full(asked_ref.shape[1:], place.astype(F32), F32)
        asked_ref[slot(rows_ref[t])] = filled

    loop(asked_ref.shape[0], one)


def prepare_kernel(
    slot,
    primal_count,
    rows_in,
    cols_in,
    steps_in,
    tiles_in,
    cot_in,
    mask_in,
    dual_mix_in,
    primal_mix_in,
    tiles_ref,
    scale_ref,
    mix_ref,
    cot_ref,
    pad_ref,
    rows_ref,
    cols_ref,
    steps_ref,
    mask_ref,
    mixes_ref,
    held_ref,
    sems,
):
    owned, channels, side = cot_ref.shape
    layers = dual_mix_in.shape[0]
    fetches = [
        pltpu.make_async_copy(source, target, sems.at[i])
        for i, (source, target) in enumerate(
            (
                (rows_in, rows_ref),
                (cols_in, cols_ref),
                (steps_in, steps_ref),
                (tiles_in, held_ref),
                (cot_in, cot_ref),
                (mask_in.at[layers - 1], mask_ref),
                (primal_mix_in, mixes_ref.at[0]),
                (dual_mix_in, mixes_ref.at[1]),
            )
        )
    ]
    for fetch in fetches:
        fetch.start()
    pad_ref[...] = jnp.zeros_like(pad_ref)
    for fetch in fetches[:3]:
        fetch.wait()
    for k in range(layers):
        for s in range(2):
            upper = jnp.full((1, side), steps_ref[k, 2 * s].astype(F32), F32)
            lower = jnp.full((1, side), steps_ref[k, 2 * s + 1].astype(F32), F32)
            scale_ref[pl.ds(2 * k + s, 1), :] = -(upper / lower)
    for fetch in fetches[6:]:
        fetch.wait()
    for k in range(layers):
        for s in range(2):
            pad_ref[2 * k + s, :, :channels] = mixes_ref[s, k]
            weights = pad_ref[2 * k + s]
            high = weights.astype(BF16).astype(F32)
            rest = weights - high
            mix_ref[2 * k + s] = (
                high
                + pltpu.roll(high, channels, 1)
                + pltpu.roll(rest, 2 * channels, 1)
                + pltpu.roll(rest, 3 * channels, 1)
            ).astype(BF16)
    for fetch in fetches[4:6]:
        fetch.wait()
    for b in range(owned):
        cot_ref[b] = mask_ref[pl.ds(b, 1), :].astype(F32) * cot_ref[b]
    fetches[3].wait()
    below = tiles_ref.shape[1] - held_ref.shape[1]

    def sort(t):
        to = slot(rows_ref[t])
        tiles_ref[to, : held_ref.shape[1], :] = held_ref[t]
        p = lax.rem(cols_ref[t], primal_count)
        filled = jnp.full((below, side), p.astype(F32), F32)
        tiles_ref[to, held_ref.shape[1] :, :] = filled.astype(BF16)

    loop(tiles_ref.shape[0], sort)


def chosen(wanted_ref, r, base):
    place = jnp.broadcast_to(wanted_ref[r], base[0].shape)
    picked = base[0]
    for b in range(1, len(base)):
        picked = jnp.where(place == b, base[b], picked)
    return picked.astype(BF16)


def choose_for_all(wanted_ref, base, send_ref):
    cols = send_ref.shape[0] // wanted_ref.shape[0]

    def one(r):
        picked = chosen(wanted_ref, r, base)
        for c in range(cols):
            send_ref[r * cols + c] = picked

    loop(wanted_ref.shape[0], one)


def first_dual_kernel(wanted_ref, cot_ref, send_ref):
    choose_for_all(wanted_ref, [cot_ref[b] for b in range(cot_ref.shape[0])], send_ref)


def sum_pushed(wanted_ref, received_ref, start):
    channels, side = start[0].shape
    rows = received_ref.shape[0]

    def step(r, blocks):
        at = jnp.broadcast_to(wanted_ref[r], (channels, side))
        pushed = received_ref[r, :channels, :].astype(F32)
        return tuple(block + jnp.where(at == b, pushed, 0.0) for b, block in enumerate(blocks))

    blocks = tuple(start)
    if rows <= 16:
        for r in range(rows):
            blocks = step(r, blocks)
        return blocks
    return lax.fori_loop(0, rows, step, blocks)


def place_of(tile, shape):
    side = tile.shape[1]
    return jnp.broadcast_to(tile[side:].astype(F32)[:1], shape)


def pushed_tile(tiles_ref, other_ref, t):
    rows = lax.axis_size("row")
    upper = lax.axis_index("row") >= rows // 2
    here = t < rows - rows // 2
    own = upper == here
    return jnp.where(own, tiles_ref[t], other_ref[t])


def mixed_by(weights, blocks):
    side = blocks[0].shape[1]
    high, rest = halves(jnp.concatenate(blocks, 1))
    mixed = jnp.dot(
        weights, jnp.concatenate([high, rest, high, rest], 0), preferred_element_type=F32
    )
    return [mixed[:, b * side : (b + 1) * side] for b in range(len(blocks))]


def folded(terms, channels):
    return terms + pltpu.roll(terms, terms.shape[1] - channels, 1)


def contract(left, right):
    return lax.dot_general(
        jnp.concatenate(left, 1),
        jnp.concatenate(right, 1),
        (((1,), (1,)), ((), ())),
        preferred_element_type=F32,
    )


def dual_kernel(
    layer,
    wanted_ref,
    received_ref,
    cot_in,
    mask_ref,
    saved_ref,
    scale_ref,
    mix_ref,
    *refs,
):
    owned, channels, side = cot_in.shape
    tiles_refs, (cot_ref, send_ref, terms_ref) = refs[:-3], refs[-3:]
    above = layer + 1
    tau = scale_ref[pl.ds(2 * above, 1), :]
    pushed = sum_pushed(
        wanted_ref, received_ref, [jnp.zeros((channels, side), F32) for _ in range(owned)]
    )
    base, left, right = [], [], []
    mixed = mixed_by(mix_ref[2 * above], pushed)
    for b in range(owned):
        block = cot_in[b] + tau * mixed[b]
        cot = mask_ref[layer, pl.ds(b, 1), :].astype(F32) * block
        cot_ref[b] = cot
        base.append(cot)
        high, rest = halves(pushed[b])
        left.append(saved_ref[above, b])
        right.append(jnp.concatenate([high, rest, high, rest], 0))
    choose_for_all(wanted_ref, base, send_ref)
    terms_ref[0] = folded(contract(left, right), channels)
    if tiles_refs:
        count = terms_ref.shape[0] - 1

        def step(t, sums):
            tile = pushed_tile(*tiles_refs, t)
            product = jnp.dot(
                received_ref[t, channels:, :], tile[:side], preferred_element_type=F32
            )
            at = place_of(tile, product.shape)
            return tuple(s + jnp.where(at == p, product, 0.0) for p, s in enumerate(sums))

        sums = tuple(jnp.zeros((channels, side), F32) for _ in range(count))
        if received_ref.shape[0] <= 16:
            for t in range(received_ref.shape[0]):
                sums = step(t, sums)
        else:
            sums = lax.fori_loop(0, received_ref.shape[0], step, sums)
        for p in range(count):
            terms_ref[1 + p] = sums[p]


def last_dual_kernel(
    row_scale,
    col_scale,
    wanted_ref,
    received_ref,
    cot_in,
    scale_ref,
    grad_in,
    grad_ref,
    cot_ref,
    primal_out,
    dual_out,
    held_ref,
    primal_ref,
    dual_ref,
    sems,
):
    owned, channels, side = held_ref.shape
    layers = primal_ref.shape[0]
    half = channels // 2
    rows = received_ref.shape[0]
    copies = [pltpu.make_async_copy(grad_in, grad_ref, sems.at[owned])]
    copies[0].start()
    blocks = sum_pushed(wanted_ref, received_ref, [cot_in[b] for b in range(owned)])
    for b, block in enumerate(blocks):
        held_ref[b] = block
        copy = pltpu.make_async_copy(held_ref.at[b], cot_ref.at[b], sems.at[b])
        copy.start()
        copies.append(copy)
    all_terms = total_of(
        rows, lambda r: received_ref[r, channels:, :].astype(F32), (layers * half, side)
    )
    for k in range(layers):
        terms = all_terms[k * half : (k + 1) * half]
        dual = scale_ref[pl.ds(2 * k + 1, 1), :] * row_scale * terms
        primal = scale_ref[pl.ds(2 * k, 1), :] * col_scale * terms
        dual_ref[k, :half, :] = dual[:, :channels]
        dual_ref[k, half:, :] = pltpu.roll(dual, side - channels, 1)[:, :channels]
        primal_ref[k, :half, :] = pltpu.roll(primal, side - 2 * channels, 1)[:, :channels]
        primal_ref[k, half:, :] = pltpu.roll(primal, side - 3 * channels, 1)[:, :channels]
    for i, (source, target) in enumerate(((primal_ref, primal_out), (dual_ref, dual_out))):
        copies.append(pltpu.make_async_copy(source, target, sems.at[owned + 1 + i]))
        copies[-1].start()
    for copy in copies:
        copy.wait()


def primal_step(layer, shared, grad_ref):
    tiles_ref, other_ref, scale_ref, mix_ref, fetched_ref, grad_in, mask_ref, saved_ref = shared
    blocks, channels, side = grad_ref.shape
    rows = tiles_ref.shape[0]
    me = lax.axis_index("col")
    sigma = scale_ref[pl.ds(2 * layer + 1, 1), :]

    def step(t, sums):
        for tiles, message in ((tiles_ref, 2 * t + 1 - me), (other_ref, 2 * t + me)):
            product = jnp.dot(
                fetched_ref[message], tiles[t, :side, :], preferred_element_type=F32
            )
            at = place_of(tiles[t], product.shape)
            sums = tuple(s + jnp.where(at == p, product, 0.0) for p, s in enumerate(sums))
        return sums

    sums = tuple(jnp.zeros((channels, side), F32) for _ in range(blocks))
    if rows <= 16:
        for t in range(rows):
            sums = step(t, sums)
    else:
        sums = lax.fori_loop(0, rows, step, sums)
    cots, extrapolated = [], []
    mixed = mixed_by(mix_ref[2 * layer + 1], sums)
    for p in range(blocks):
        back = sigma * mixed[p]
        cot = mask_ref[layer, pl.ds(p, 1), :].astype(F32) * (grad_in[p] + 2.0 * back)
        grad_ref[p] = cot - back
        cots.append(cot)
        extrapolated.append(
            (
                2.0 * saved_ref[layer + 1, p].astype(F32) - saved_ref[layer, p].astype(F32)
            ).astype(BF16)
        )
    return sums, cots, extrapolated


def push(tiles_ref, other_ref, blocks, send_ref, below):
    channels, side = blocks[0].shape

    def one(t):
        tile = pushed_tile(tiles_ref, other_ref, t)
        at = place_of(tile, blocks[0].shape)
        picked = blocks[0]
        for p in range(1, len(blocks)):
            picked = jnp.where(at == p, blocks[p], picked)
        product = lax.dot_general(
            picked.astype(BF16),
            tile[:side],
            (((1,), (1,)), ((), ())),
            preferred_element_type=F32,
        )
        send_ref[t, :channels, :] = product.astype(BF16)
        if below is not None:
            send_ref[t, channels:, :] = below(t)

    loop(tiles_ref.shape[0], one)


def primal_kernel(layer, *refs):
    shared, rest, (grad_ref, send_ref, terms_ref) = refs[:8], refs[8:-3], refs[-3:]
    blocks, channels, side = grad_ref.shape
    sums, cots, extrapolated = primal_step(layer, shared, grad_ref)
    below = None
    if rest:
        wanted_ref, dual_ref = rest
        base = [dual_ref[0, b].astype(F32) for b in range(dual_ref.shape[1])]
        below = lambda t: chosen(wanted_ref, t, base)
    push(*shared[:2], cots, send_ref, below)
    right = []
    for p in range(blocks):
        high, low = halves(sums[p])
        right.append(jnp.concatenate([high, low, high, low], 0))
    terms_ref[...] = folded(contract(extrapolated, right), channels)


def last_primal_kernel(*refs):
    shared, rest, (grad_ref, send_ref) = refs[:8], refs[8:-2], refs[-2:]
    early_ref, early_other, late_ref, late_other, *dual_terms = rest
    scale_ref, mix_ref = shared[2], shared[3]
    blocks, channels, side = grad_ref.shape
    half = channels // 2
    sums, cots, extrapolated = primal_step(0, shared, grad_ref)
    tau = scale_ref[pl.ds(0, 1), :]
    left, right = [], []
    for p in range(blocks):
        pulled = early_ref[1 + p] + early_other[1 + p]
        left.append(jnp.concatenate([extrapolated[p], *halves(pulled)], 0))
        right.append(jnp.concatenate([*halves(sums[p]), *halves(cots[p])], 0))
    terms = contract(left, right)
    lane = lax.broadcasted_iota(jnp.int32, (channels, side), 1)
    low = lane < 2 * channels
    terms = jnp.where(
        low, terms[:channels], terms[channels : 2 * channels] + terms[2 * channels :]
    )
    primal_terms = (late_ref[0] + late_other[0], early_ref[0] + early_other[0])
    all_terms = [folded(terms, channels)] + [
        jnp.where(low, dual[...], primal) for dual, primal in zip(dual_terms, primal_terms)
    ]
    packed = jnp.concatenate(
        [
            jnp.where(
                lax.rem(lane[:half], 2 * channels) < channels,
                one[:half],
                pltpu.roll(one[half:], channels, 1),
            )
            for one in all_terms
        ],
        0,
    ).astype(BF16)
    mixed = [
        (tau * cot).astype(BF16).astype(F32) for cot in mixed_by(mix_ref[0], cots)
    ]
    push(*shared[:2], mixed, send_ref, lambda t: packed)


def per_device(
    tile_blocks,
    tile_rows,
    tile_cols,
    saved_primal,
    saved_dual,
    primal_active,
    dual_active,
    primal_mix,
    dual_mix,
    step_fracs,
    cot_primal,
    cot_dual,
):
    row_count = lax.axis_size("row")
    col_count = lax.axis_size("col")
    owned, channels, side = cot_dual.shape
    primal_count = cot_primal.shape[0]
    layer_count = primal_mix.shape[0]
    half = channels // 2
    row_scale = 1.0 / math.sqrt(owned * row_count * col_count * side)
    col_scale = 1.0 / math.sqrt(primal_count * row_count * side)
    params = pltpu.CompilerParams(vmem_limit_bytes=24 * 1024 * 1024)

    def call(kernel, outs, *operands, ins=None, out_specs=None, **rest):
        return pl.pallas_call(
            kernel,
            out_shape=outs,
            in_specs=ins or [VMEM] * len(operands),
            out_specs=out_specs or jax.tree.map(lambda _: VMEM, outs),
            compiler_params=params,
            **rest,
        )(*operands)

    shift = row_count - row_count // 2
    order = [(slot + row_count - shift) % row_count for slot in range(row_count)]
    order_all = [row * col_count + c for row in order for c in reversed(range(col_count))]

    order_push = [
        [
            row * col_count + (c if i < shift else col_count - 1 - c)
            for i, row in enumerate(order)
        ]
        for c in range(col_count)
    ]

    def exchange(x, axes, groups):
        return lax.all_to_all(
            x, axes, split_axis=0, concat_axis=0, axis_index_groups=groups, tiled=True
        )

    def shape(dims, kind=F32):
        return jax.ShapeDtypeStruct(dims, kind)

    def in_hbm(*arrays):
        return [pltpu.with_memory_space_constraint(x, pltpu.HBM) for x in arrays]

    def swap(x):
        return lax.ppermute(x, "col", [(i, col_count - 1 - i) for i in range(col_count)])

    slot = partial(slot_of, peer_size=owned * col_count, shift=shift, row_count=row_count)
    asked = call(
        partial(ask_kernel, slot, owned),
        shape((row_count, 1, side)),
        *in_hbm(tile_rows),
        ins=[HBM],
        scratch_shapes=[pltpu.SMEM(tile_rows.shape, jnp.int32), pltpu.SemaphoreType.DMA],
    )
    wanted = exchange(asked, "row", [order])
    tiles, scale, mix, cot = call(
        partial(prepare_kernel, slot, primal_count),
        (
            shape((row_count, side + 16, side), BF16),
            shape((2 * layer_count, side)),
            shape((2 * layer_count, channels, side), BF16),
            shape(cot_dual.shape),
        ),
        *in_hbm(
            tile_rows,
            tile_cols,
            step_fracs,
            tile_blocks,
            cot_dual,
            dual_active,
            dual_mix,
            primal_mix,
        ),
        ins=[HBM] * 8,
        scratch_shapes=[
            pltpu.VMEM((2 * layer_count, channels, side), F32),
            pltpu.SMEM(tile_rows.shape, jnp.int32),
            pltpu.SMEM(tile_cols.shape, jnp.int32),
            pltpu.SMEM(step_fracs.shape, jnp.int32),
            pltpu.VMEM((owned, side), jnp.int32),
            pltpu.VMEM((2, layer_count, channels, channels), F32),
            pltpu.VMEM(tile_blocks.shape, BF16),
            pltpu.SemaphoreType.DMA((8,)),
        ],
    )
    other_tiles = swap(lax.optimization_barrier((tiles, wanted))[0])
    blocks_out = shape((col_count * row_count, channels, side), BF16)
    grad_x = cot_primal
    send = call(first_dual_kernel, blocks_out, wanted, cot)
    dual_terms, primal_terms = [], []
    for layer in reversed(range(layer_count)):
        fetched = exchange(send, ("row", "col"), [order_all])
        shared = (
            tiles,
            other_tiles,
            scale,
            mix,
            fetched,
            grad_x,
            primal_active,
            saved_primal,
        )
        if layer == 0:
            height = channels + layer_count * half
            grad_x, pushed = call(
                last_primal_kernel,
                (shape(cot_primal.shape), shape((row_count, height, side), BF16)),
                *shared,
                *primal_terms,
                *dual_terms[::-1],
            )
            received = exchange(pushed, ("row", "col"), order_push)
            break
        first = layer == layer_count - 1
        height = 2 * channels if first else channels
        grad_x, pushed, terms = call(
            partial(primal_kernel, layer),
            (
                shape(cot_primal.shape),
                shape((row_count, height, side), BF16),
                shape((channels, side)),
            ),
            *shared,
            *((wanted, saved_dual) if first else ()),
        )
        dual_terms.append(terms)
        received = exchange(pushed, ("row", "col"), order_push)
        cot, send, terms = call(
            partial(dual_kernel, layer - 1),
            (
                shape(cot_dual.shape),
                blocks_out,
                shape((1 + (primal_count if first else 0), channels, side)),
            ),
            wanted,
            received,
            cot,
            dual_active,
            saved_dual,
            scale,
            mix,
            *((tiles, other_tiles) if first else ()),
        )
        primal_terms += [terms, swap(terms)]
    grad_x, grad_y, primal_mix_grad, dual_mix_grad = call(
        partial(last_dual_kernel, row_scale, col_scale),
        (
            shape(cot_primal.shape),
            shape(cot_dual.shape),
            shape(primal_mix.shape),
            shape(dual_mix.shape),
        ),
        wanted,
        received,
        cot,
        scale,
        grad_x,
        out_specs=(HBM,) * 4,
        scratch_shapes=[
            pltpu.VMEM(cot_dual.shape, F32),
            pltpu.VMEM(primal_mix.shape, F32),
            pltpu.VMEM(dual_mix.shape, F32),
            pltpu.SemaphoreType.DMA((owned + 3,)),
        ],
    )
    return (grad_x, grad_y, primal_mix_grad, dual_mix_grad)


def solution(mesh):
    return jax.shard_map(
        per_device,
        mesh=mesh,
        in_specs=(
            P(("groups", "row", "col"), None, None),
            P(("groups", "row", "col")),
            P(("groups", "row", "col")),
            P(None, ("groups", "row"), None, None),
            P(None, ("groups", "row", "col"), None, None),
            P(None, ("groups", "row"), None),
            P(None, ("groups", "row", "col"), None),
            P(),
            P(),
            P(),
            P(("groups", "row"), None, None),
            P(("groups", "row", "col"), None, None),
        ),
        out_specs=(
            P(("groups", "row"), None, None),
            P(("groups", "row", "col"), None, None),
            P("groups", None, None),
            P("groups", None, None),
        ),
        check_vma=False,
    )
```

```python
from functools import partial
import math

import jax
import jax.numpy as jnp
from jax import lax
from jax.experimental import pallas as pl
from jax.experimental.pallas import tpu as pltpu
from jax.sharding import PartitionSpec as P

VMEM = pl.BlockSpec(memory_space=pltpu.VMEM)
HBM = pl.BlockSpec(memory_space=pltpu.HBM)
F32 = jnp.float32
BF16 = jnp.bfloat16


def loop(count, body):
    if count <= 16:
        for i in range(count):
            body(i)
    else:
        lax.fori_loop(0, count, lambda i, _: (body(i), 0)[1], 0)


def total_of(count, term, shape):
    if count <= 16:
        total = term(0)
        for i in range(1, count):
            total = total + term(i)
        return total
    return lax.fori_loop(0, count, lambda i, t: t + term(i), jnp.zeros(shape, F32))


def halves(x):
    high = x.astype(BF16)
    return high, (x - high.astype(F32)).astype(BF16)


def slot_of(row, peer_size, shift, row_count):
    return lax.rem(lax.div(row, peer_size) + shift, row_count)


def ask_kernel(slot, owned, rows_in, asked_ref, rows_ref, sem):
    fetch = pltpu.make_async_copy(rows_in, rows_ref, sem)
    fetch.start()
    fetch.wait()

    def one(t):
        place = lax.rem(rows_ref[t], owned)
        filled = jnp.full(asked_ref.shape[1:], place.astype(F32), F32)
        asked_ref[slot(rows_ref[t])] = filled

    loop(asked_ref.shape[0], one)


def prepare_kernel(
    slot,
    primal_count,
    rows_in,
    cols_in,
    steps_in,
    tiles_in,
    cot_in,
    mask_in,
    dual_mix_in,
    primal_mix_in,
    tiles_ref,
    scale_ref,
    mix_ref,
    cot_ref,
    pad_ref,
    rows_ref,
    cols_ref,
    steps_ref,
    mask_ref,
    mixes_ref,
    held_ref,
    sems,
):
    owned, channels, side = cot_ref.shape
    layers = dual_mix_in.shape[0]
    fetches = [
        pltpu.make_async_copy(source, target, sems.at[i])
        for i, (source, target) in enumerate(
            (
                (rows_in, rows_ref),
                (cols_in, cols_ref),
                (steps_in, steps_ref),
                (tiles_in, held_ref),
                (cot_in, cot_ref),
                (mask_in.at[layers - 1], mask_ref),
                (primal_mix_in, mixes_ref.at[0]),
                (dual_mix_in, mixes_ref.at[1]),
            )
        )
    ]
    for fetch in fetches:
        fetch.start()
    pad_ref[...] = jnp.zeros_like(pad_ref)
    for fetch in fetches[:3]:
        fetch.wait()
    for k in range(layers):
        for s in range(2):
            upper = jnp.full((1, side), steps_ref[k, 2 * s].astype(F32), F32)
            lower = jnp.full((1, side), steps_ref[k, 2 * s + 1].astype(F32), F32)
            scale_ref[pl.ds(2 * k + s, 1), :] = -(upper / lower)
    for fetch in fetches[6:]:
        fetch.wait()
    for k in range(layers):
        for s in range(2):
            pad_ref[2 * k + s, :, :channels] = mixes_ref[s, k]
            weights = pad_ref[2 * k + s]
            high = weights.astype(BF16).astype(F32)
            rest = weights - high
            mix_ref[2 * k + s] = (
                high
                + pltpu.roll(high, channels, 1)
                + pltpu.roll(rest, 2 * channels, 1)
                + pltpu.roll(rest, 3 * channels, 1)
            ).astype(BF16)
    for fetch in fetches[4:6]:
        fetch.wait()
    for b in range(owned):
        cot_ref[b] = mask_ref[pl.ds(b, 1), :].astype(F32) * cot_ref[b]
    fetches[3].wait()
    below = tiles_ref.shape[1] - held_ref.shape[1]

    def sort(t):
        to = slot(rows_ref[t])
        tiles_ref[to, : held_ref.shape[1], :] = held_ref[t]
        p = lax.rem(cols_ref[t], primal_count)
        filled = jnp.full((below, side), p.astype(F32), F32)
        tiles_ref[to, held_ref.shape[1] :, :] = filled.astype(BF16)

    loop(tiles_ref.shape[0], sort)


def chosen(wanted_ref, r, base):
    place = jnp.broadcast_to(wanted_ref[r], base[0].shape)
    picked = base[0]
    for b in range(1, len(base)):
        picked = jnp.where(place == b, base[b], picked)
    return picked.astype(BF16)


def choose_for_all(wanted_ref, base, send_ref):
    cols = send_ref.shape[0] // wanted_ref.shape[0]

    def one(r):
        picked = chosen(wanted_ref, r, base)
        for c in range(cols):
            send_ref[r * cols + c] = picked

    loop(wanted_ref.shape[0], one)


def first_dual_kernel(wanted_ref, cot_ref, send_ref):
    choose_for_all(wanted_ref, [cot_ref[b] for b in range(cot_ref.shape[0])], send_ref)


def sum_pushed(wanted_ref, received_ref, start):
    channels, side = start[0].shape
    rows = received_ref.shape[0]

    def step(r, blocks):
        at = jnp.broadcast_to(wanted_ref[r], (channels, side))
        pushed = received_ref[r, :channels, :].astype(F32)
        return tuple(block + jnp.where(at == b, pushed, 0.0) for b, block in enumerate(blocks))

    blocks = tuple(start)
    if rows <= 16:
        for r in range(rows):
            blocks = step(r, blocks)
        return blocks
    return lax.fori_loop(0, rows, step, blocks)


def place_of(tile, shape):
    side = tile.shape[1]
    return jnp.broadcast_to(tile[side:].astype(F32)[:1], shape)


def pushed_tile(tiles_ref, other_ref, t):
    rows = lax.axis_size("row")
    upper = lax.axis_index("row") >= rows // 2
    here = t < rows - rows // 2
    own = upper == here
    return jnp.where(own, tiles_ref[t], other_ref[t])


def mixed_by(weights, blocks):
    side = blocks[0].shape[1]
    high, rest = halves(jnp.concatenate(blocks, 1))
    mixed = jnp.dot(
        weights, jnp.concatenate([high, rest, high, rest], 0), preferred_element_type=F32
    )
    return [mixed[:, b * side : (b + 1) * side] for b in range(len(blocks))]


def folded(terms, channels):
    return terms + pltpu.roll(terms, terms.shape[1] - channels, 1)


def contract(left, right):
    return lax.dot_general(
        jnp.concatenate(left, 1),
        jnp.concatenate(right, 1),
        (((1,), (1,)), ((), ())),
        preferred_element_type=F32,
    )


def dual_step(layer, pushed, cot_in, mask_ref, scale_ref, mix_ref, wanted_ref, cot_ref, send_ref):
    above = layer + 1
    tau = scale_ref[pl.ds(2 * above, 1), :]
    mixed = mixed_by(mix_ref[2 * above], pushed)
    base = []
    for b in range(len(pushed)):
        cot = mask_ref[layer, pl.ds(b, 1), :].astype(F32) * (cot_in[b] + tau * mixed[b])
        cot_ref[b] = cot
        base.append(cot)
    choose_for_all(wanted_ref, base, send_ref)


def all_pushed(wanted_ref, received_ref, pushed_ref):
    owned, channels, side = pushed_ref.shape
    pushed = sum_pushed(
        wanted_ref, received_ref, [jnp.zeros((channels, side), F32) for _ in range(owned)]
    )
    for b in range(owned):
        pushed_ref[b] = pushed[b]
    return pushed


def dual_kernel(layer, received_ref, *refs):
    *refs, pushed_ref = refs
    wanted_ref = refs[4]
    dual_step(layer, all_pushed(wanted_ref, received_ref, pushed_ref), *refs)


def last_layer_dual_kernel(pushed_ref, *refs):
    dual_step(0, [pushed_ref[b] for b in range(pushed_ref.shape[0])], *refs)


def doubled_halves(x):
    high, rest = halves(x)
    return jnp.concatenate([high, rest, high, rest], 0)


def extrapolate(saved_ref, layer, p):
    return (
        2.0 * saved_ref[layer + 1, p].astype(F32) - saved_ref[layer, p].astype(F32)
    ).astype(BF16)


def terms_kernel(
    wanted_ref,
    last_received_ref,
    saved_dual_ref,
    saved_primal_ref,
    tiles_ref,
    other_ref,
    received_ref,
    *refs,
):
    last_sums_ref, last_pushed_ref, part_ref, dual_ref = refs[-4:]
    refs = (*refs[:-4], last_pushed_ref, last_sums_ref)
    early, channels, side = dual_ref.shape
    owned, blocks = saved_dual_ref.shape[1], saved_primal_ref.shape[1]
    all_pushed(wanted_ref, last_received_ref, last_pushed_ref)
    for i in range(early):
        pushed_ref, sums_ref = refs[2 * i], refs[2 * i + 1]
        layer = early - i
        part_ref[layer - 1] = folded(
            contract(
                [saved_dual_ref[layer, b] for b in range(owned)],
                [doubled_halves(pushed_ref[b]) for b in range(owned)],
            ),
            channels,
        )
        dual_ref[layer - 1] = folded(
            contract(
                [extrapolate(saved_primal_ref, layer, p) for p in range(blocks)],
                [doubled_halves(sums_ref[p]) for p in range(blocks)],
            ),
            channels,
        )

    def step(t, sums):
        tile = pushed_tile(tiles_ref, other_ref, t)
        product = jnp.dot(
            received_ref[t, channels:, :], tile[:side], preferred_element_type=F32
        )
        at = place_of(tile, product.shape)
        return tuple(s + jnp.where(at == p, product, 0.0) for p, s in enumerate(sums))

    sums = tuple(jnp.zeros((channels, side), F32) for _ in range(blocks))
    if received_ref.shape[0] <= 16:
        for t in range(received_ref.shape[0]):
            sums = step(t, sums)
    else:
        sums = lax.fori_loop(0, received_ref.shape[0], step, sums)
    for p in range(blocks):
        part_ref[early + p] = sums[p]
    for i in range(early + blocks, part_ref.shape[0]):
        part_ref[i] = jnp.zeros((channels, side), F32)


def last_dual_kernel(
    row_scale,
    col_scale,
    wanted_ref,
    received_ref,
    cot_in,
    scale_ref,
    grad_in,
    grad_ref,
    cot_ref,
    primal_out,
    dual_out,
    held_ref,
    primal_ref,
    dual_ref,
    sems,
):
    owned, channels, side = held_ref.shape
    layers = primal_ref.shape[0]
    half = channels // 2
    rows = received_ref.shape[0]
    copies = [pltpu.make_async_copy(grad_in, grad_ref, sems.at[owned])]
    copies[0].start()
    blocks = sum_pushed(wanted_ref, received_ref, [cot_in[b] for b in range(owned)])
    for b, block in enumerate(blocks):
        held_ref[b] = block
        copy = pltpu.make_async_copy(held_ref.at[b], cot_ref.at[b], sems.at[b])
        copy.start()
        copies.append(copy)
    all_terms = total_of(
        rows, lambda r: received_ref[r, channels:, :].astype(F32), (layers * half, side)
    )
    for k in range(layers):
        terms = all_terms[k * half : (k + 1) * half]
        dual = scale_ref[pl.ds(2 * k + 1, 1), :] * row_scale * terms
        primal = scale_ref[pl.ds(2 * k, 1), :] * col_scale * terms
        dual_ref[k, :half, :] = dual[:, :channels]
        dual_ref[k, half:, :] = pltpu.roll(dual, side - channels, 1)[:, :channels]
        primal_ref[k, :half, :] = pltpu.roll(primal, side - 2 * channels, 1)[:, :channels]
        primal_ref[k, half:, :] = pltpu.roll(primal, side - 3 * channels, 1)[:, :channels]
    for i, (source, target) in enumerate(((primal_ref, primal_out), (dual_ref, dual_out))):
        copies.append(pltpu.make_async_copy(source, target, sems.at[owned + 1 + i]))
        copies[-1].start()
    for copy in copies:
        copy.wait()


def primal_step(layer, shared, grad_ref):
    tiles_ref, other_ref, scale_ref, mix_ref, fetched_ref, grad_in, mask_ref = shared
    blocks, channels, side = grad_ref.shape
    rows = tiles_ref.shape[0]
    me = lax.axis_index("col")
    sigma = scale_ref[pl.ds(2 * layer + 1, 1), :]

    def step(t, sums):
        for tiles, message in ((tiles_ref, 2 * t + 1 - me), (other_ref, 2 * t + me)):
            product = jnp.dot(
                fetched_ref[message], tiles[t, :side, :], preferred_element_type=F32
            )
            at = place_of(tiles[t], product.shape)
            sums = tuple(s + jnp.where(at == p, product, 0.0) for p, s in enumerate(sums))
        return sums

    sums = tuple(jnp.zeros((channels, side), F32) for _ in range(blocks))
    if rows <= 16:
        for t in range(rows):
            sums = step(t, sums)
    else:
        sums = lax.fori_loop(0, rows, step, sums)
    cots = []
    mixed = mixed_by(mix_ref[2 * layer + 1], sums)
    for p in range(blocks):
        back = sigma * mixed[p]
        cot = mask_ref[layer, pl.ds(p, 1), :].astype(F32) * (grad_in[p] + 2.0 * back)
        grad_ref[p] = cot - back
        cots.append(cot)
    return sums, cots


def push(tiles_ref, other_ref, blocks, send_ref, below):
    channels, side = blocks[0].shape

    def one(t):
        tile = pushed_tile(tiles_ref, other_ref, t)
        at = place_of(tile, blocks[0].shape)
        picked = blocks[0]
        for p in range(1, len(blocks)):
            picked = jnp.where(at == p, blocks[p], picked)
        product = lax.dot_general(
            picked.astype(BF16),
            tile[:side],
            (((1,), (1,)), ((), ())),
            preferred_element_type=F32,
        )
        send_ref[t, :channels, :] = product.astype(BF16)
        if below is not None:
            send_ref[t, channels:, :] = below(t)

    loop(tiles_ref.shape[0], one)


def primal_kernel(layer, *refs):
    shared, rest, (grad_ref, send_ref, sums_ref) = refs[:7], refs[7:-3], refs[-3:]
    sums, cots = primal_step(layer, shared, grad_ref)
    below = None
    if rest:
        wanted_ref, dual_ref = rest
        base = [dual_ref[0, b].astype(F32) for b in range(dual_ref.shape[1])]
        below = lambda t: chosen(wanted_ref, t, base)
    push(*shared[:2], cots, send_ref, below)
    for p, total in enumerate(sums):
        sums_ref[p] = total


def last_primal_kernel(*refs):
    shared, rest, (grad_ref, send_ref) = refs[:7], refs[7:-2], refs[-2:]
    saved_ref, part_ref, part_other, dual_ref = rest
    scale_ref, mix_ref = shared[2], shared[3]
    blocks, channels, side = grad_ref.shape
    early = dual_ref.shape[0]
    half = channels // 2
    sums, cots = primal_step(0, shared, grad_ref)
    tau = scale_ref[pl.ds(0, 1), :]
    left, right = [], []
    for p in range(blocks):
        pulled = part_ref[early + p] + part_other[early + p]
        left.append(jnp.concatenate([extrapolate(saved_ref, 0, p), *halves(pulled)], 0))
        right.append(jnp.concatenate([*halves(sums[p]), *halves(cots[p])], 0))
    terms = contract(left, right)
    lane = lax.broadcasted_iota(jnp.int32, (channels, side), 1)
    low = lane < 2 * channels
    terms = jnp.where(
        low, terms[:channels], terms[channels : 2 * channels] + terms[2 * channels :]
    )
    all_terms = [folded(terms, channels)] + [
        jnp.where(low, dual_ref[i], part_ref[i] + part_other[i]) for i in range(early)
    ]
    packed = jnp.concatenate(
        [
            jnp.where(
                lax.rem(lane[:half], 2 * channels) < channels,
                one[:half],
                pltpu.roll(one[half:], channels, 1),
            )
            for one in all_terms
        ],
        0,
    ).astype(BF16)
    mixed = [
        (tau * cot).astype(BF16).astype(F32) for cot in mixed_by(mix_ref[0], cots)
    ]
    push(*shared[:2], mixed, send_ref, lambda t: packed)


def per_device(
    tile_blocks,
    tile_rows,
    tile_cols,
    saved_primal,
    saved_dual,
    primal_active,
    dual_active,
    primal_mix,
    dual_mix,
    step_fracs,
    cot_primal,
    cot_dual,
):
    row_count = lax.axis_size("row")
    col_count = lax.axis_size("col")
    owned, channels, side = cot_dual.shape
    primal_count = cot_primal.shape[0]
    layer_count = primal_mix.shape[0]
    half = channels // 2
    row_scale = 1.0 / math.sqrt(owned * row_count * col_count * side)
    col_scale = 1.0 / math.sqrt(primal_count * row_count * side)
    params = pltpu.CompilerParams(vmem_limit_bytes=24 * 1024 * 1024)

    def call(kernel, outs, *operands, ins=None, out_specs=None, **rest):
        return pl.pallas_call(
            kernel,
            out_shape=outs,
            in_specs=ins or [VMEM] * len(operands),
            out_specs=out_specs or jax.tree.map(lambda _: VMEM, outs),
            compiler_params=params,
            **rest,
        )(*operands)

    shift = row_count - row_count // 2
    order = [(slot + row_count - shift) % row_count for slot in range(row_count)]
    order_all = [row * col_count + c for row in order for c in reversed(range(col_count))]

    order_push = [
        [
            row * col_count + (c if i < shift else col_count - 1 - c)
            for i, row in enumerate(order)
        ]
        for c in range(col_count)
    ]

    def exchange(x, axes, groups):
        return lax.all_to_all(
            x, axes, split_axis=0, concat_axis=0, axis_index_groups=groups, tiled=True
        )

    def shape(dims, kind=F32):
        return jax.ShapeDtypeStruct(dims, kind)

    def in_hbm(*arrays):
        return [pltpu.with_memory_space_constraint(x, pltpu.HBM) for x in arrays]

    def swap(x):
        return lax.ppermute(x, "col", [(i, col_count - 1 - i) for i in range(col_count)])

    slot = partial(slot_of, peer_size=owned * col_count, shift=shift, row_count=row_count)
    asked = call(
        partial(ask_kernel, slot, owned),
        shape((row_count, 1, side)),
        *in_hbm(tile_rows),
        ins=[HBM],
        scratch_shapes=[pltpu.SMEM(tile_rows.shape, jnp.int32), pltpu.SemaphoreType.DMA],
    )
    wanted = exchange(asked, "row", [order])
    tiles, scale, mix, cot = call(
        partial(prepare_kernel, slot, primal_count),
        (
            shape((row_count, side + 16, side), BF16),
            shape((2 * layer_count, side)),
            shape((2 * layer_count, channels, side), BF16),
            shape(cot_dual.shape),
        ),
        *in_hbm(
            tile_rows,
            tile_cols,
            step_fracs,
            tile_blocks,
            cot_dual,
            dual_active,
            dual_mix,
            primal_mix,
        ),
        ins=[HBM] * 8,
        scratch_shapes=[
            pltpu.VMEM((2 * layer_count, channels, side), F32),
            pltpu.SMEM(tile_rows.shape, jnp.int32),
            pltpu.SMEM(tile_cols.shape, jnp.int32),
            pltpu.SMEM(step_fracs.shape, jnp.int32),
            pltpu.VMEM((owned, side), jnp.int32),
            pltpu.VMEM((2, layer_count, channels, channels), F32),
            pltpu.VMEM(tile_blocks.shape, BF16),
            pltpu.SemaphoreType.DMA((8,)),
        ],
    )
    other_tiles = swap(lax.optimization_barrier((tiles, wanted))[0])
    blocks_out = shape((col_count * row_count, channels, side), BF16)
    grad_x = cot_primal
    send = call(first_dual_kernel, blocks_out, wanted, cot)
    carried = []
    first_received = None
    spread = 16
    for layer in reversed(range(layer_count)):
        fetched = exchange(send, ("row", "col"), [order_all])
        shared = (tiles, other_tiles, scale, mix, fetched, grad_x, primal_active)
        if layer == 0:
            height = channels + layer_count * half
            grad_x, pushed = call(
                last_primal_kernel,
                (shape(cot_primal.shape), shape((row_count, height, side), BF16)),
                *shared,
                saved_primal,
                part,
                part_other,
                dual_terms,
            )
            received = exchange(pushed, ("row", "col"), order_push)
            break
        first = layer == layer_count - 1
        height = 2 * channels if first else channels
        grad_x, pushed, sums = call(
            partial(primal_kernel, layer),
            (
                shape(cot_primal.shape),
                shape((row_count, height, side), BF16),
                shape(cot_primal.shape),
            ),
            *shared,
            *((wanted, saved_dual) if first else ()),
        )
        received = exchange(pushed, ("row", "col"), order_push)
        if first:
            first_received = received
        state = (cot, dual_active, scale, mix, wanted)
        dual_shape = shape(cot_dual.shape)
        if layer > 1:
            cot, send, sums_pushed = call(
                partial(dual_kernel, layer - 1),
                (dual_shape, blocks_out, dual_shape),
                received,
                *state,
            )
            carried += [sums_pushed, sums]
            continue
        sums_pushed, part, dual_terms = call(
            terms_kernel,
            (
                dual_shape,
                shape((max(spread, layer_count - 1 + primal_count), channels, side)),
                shape((layer_count - 1, channels, side)),
            ),
            wanted,
            received,
            saved_dual,
            saved_primal,
            tiles,
            other_tiles,
            first_received,
            *carried,
            sums,
        )
        part_other = swap(part)
        cot, send = call(last_layer_dual_kernel, (dual_shape, blocks_out), sums_pushed, *state)
    grad_x, grad_y, primal_mix_grad, dual_mix_grad = call(
        partial(last_dual_kernel, row_scale, col_scale),
        (
            shape(cot_primal.shape),
            shape(cot_dual.shape),
            shape(primal_mix.shape),
            shape(dual_mix.shape),
        ),
        wanted,
        received,
        cot,
        scale,
        grad_x,
        out_specs=(HBM,) * 4,
        scratch_shapes=[
            pltpu.VMEM(cot_dual.shape, F32),
            pltpu.VMEM(primal_mix.shape, F32),
            pltpu.VMEM(dual_mix.shape, F32),
            pltpu.SemaphoreType.DMA((owned + 3,)),
        ],
    )
    return (grad_x, grad_y, primal_mix_grad, dual_mix_grad)


def solution(mesh):
    return jax.shard_map(
        per_device,
        mesh=mesh,
        in_specs=(
            P(("groups", "row", "col"), None, None),
            P(("groups", "row", "col")),
            P(("groups", "row", "col")),
            P(None, ("groups", "row"), None, None),
            P(None, ("groups", "row", "col"), None, None),
            P(None, ("groups", "row"), None),
            P(None, ("groups", "row", "col"), None),
            P(),
            P(),
            P(),
            P(("groups", "row"), None, None),
            P(("groups", "row", "col"), None, None),
        ),
        out_specs=(
            P(("groups", "row"), None, None),
            P(("groups", "row", "col"), None, None),
            P("groups", None, None),
            P("groups", None, None),
        ),
        check_vma=False,
    )
```

```python
from functools import partial
import math

import jax
import jax.numpy as jnp
from jax import lax
from jax.experimental import pallas as pl
from jax.experimental.pallas import tpu as pltpu
from jax.sharding import PartitionSpec as P

VMEM = pl.BlockSpec(memory_space=pltpu.VMEM)
HBM = pl.BlockSpec(memory_space=pltpu.HBM)
F32 = jnp.float32
BF16 = jnp.bfloat16


def loop(count, body):
    if count <= 16:
        for i in range(count):
            body(i)
    else:
        lax.fori_loop(0, count, lambda i, _: (body(i), 0)[1], 0)


def total_of(count, term, shape):
    if count <= 16:
        total = term(0)
        for i in range(1, count):
            total = total + term(i)
        return total
    return lax.fori_loop(0, count, lambda i, t: t + term(i), jnp.zeros(shape, F32))


def halves(x):
    high = x.astype(BF16)
    return high, (x - high.astype(F32)).astype(BF16)


def slot_of(row, peer_size, shift, row_count):
    return lax.rem(lax.div(row, peer_size) + shift, row_count)


def spot_of(order, order_all, col_count, slot, col):
    if not isinstance(slot, int):
        return slot * col_count + col_count - 1 - col
    spots = [order_all.index(order[slot] * col_count + c) for c in range(col_count)]
    if isinstance(col, int):
        return spots[col]
    return sum(jnp.where(col == c, spot, 0) for c, spot in enumerate(spots))


def ask_kernel(slot, owned, rows_in, asked_ref, rows_ref, sem):
    fetch = pltpu.make_async_copy(rows_in, rows_ref, sem)
    fetch.start()
    fetch.wait()

    def one(t):
        place = lax.rem(rows_ref[t], owned)
        filled = jnp.full(asked_ref.shape[1:], place.astype(F32), F32)
        asked_ref[slot(rows_ref[t])] = filled

    loop(asked_ref.shape[0], one)


def prepare_kernel(
    slot,
    primal_count,
    rows_in,
    cols_in,
    steps_in,
    tiles_in,
    cot_in,
    mask_in,
    dual_mix_in,
    primal_mix_in,
    tiles_ref,
    scale_ref,
    mix_ref,
    cot_ref,
    pad_ref,
    rows_ref,
    cols_ref,
    steps_ref,
    mask_ref,
    mixes_ref,
    held_ref,
    sems,
):
    owned, channels, side = cot_ref.shape
    layers = dual_mix_in.shape[0]
    fetches = [
        pltpu.make_async_copy(source, target, sems.at[i])
        for i, (source, target) in enumerate(
            (
                (rows_in, rows_ref),
                (cols_in, cols_ref),
                (steps_in, steps_ref),
                (tiles_in, held_ref),
                (cot_in, cot_ref),
                (mask_in.at[layers - 1], mask_ref),
                (primal_mix_in, mixes_ref.at[0]),
                (dual_mix_in, mixes_ref.at[1]),
            )
        )
    ]
    for fetch in fetches:
        fetch.start()
    pad_ref[...] = jnp.zeros_like(pad_ref)
    for fetch in fetches[:3]:
        fetch.wait()
    for k in range(layers):
        for s in range(2):
            upper = jnp.full((1, side), steps_ref[k, 2 * s].astype(F32), F32)
            lower = jnp.full((1, side), steps_ref[k, 2 * s + 1].astype(F32), F32)
            scale_ref[pl.ds(2 * k + s, 1), :] = -(upper / lower)
    for fetch in fetches[6:]:
        fetch.wait()
    for k in range(layers):
        for s in range(2):
            pad_ref[2 * k + s, :, :channels] = mixes_ref[s, k]
            weights = pad_ref[2 * k + s]
            high = weights.astype(BF16).astype(F32)
            rest = weights - high
            mix_ref[2 * k + s] = (
                high
                + pltpu.roll(high, channels, 1)
                + pltpu.roll(rest, 2 * channels, 1)
                + pltpu.roll(rest, 3 * channels, 1)
            ).astype(BF16)
    for fetch in fetches[4:6]:
        fetch.wait()
    for b in range(owned):
        cot_ref[b] = mask_ref[pl.ds(b, 1), :].astype(F32) * cot_ref[b]
    fetches[3].wait()
    below = tiles_ref.shape[1] - held_ref.shape[1]

    def sort(t):
        to = slot(rows_ref[t])
        tiles_ref[to, : held_ref.shape[1], :] = held_ref[t]
        p = lax.rem(cols_ref[t], primal_count)
        filled = jnp.full((below, side), p.astype(F32), F32)
        tiles_ref[to, held_ref.shape[1] :, :] = filled.astype(BF16)

    loop(tiles_ref.shape[0], sort)


def chosen(wanted_ref, r, base):
    place = jnp.broadcast_to(wanted_ref[r], base[0].shape)
    picked = base[0]
    for b in range(1, len(base)):
        picked = jnp.where(place == b, base[b], picked)
    return picked.astype(BF16)


def choose_for_all(spot, wanted_ref, base, send_ref):
    cols = send_ref.shape[0] // wanted_ref.shape[0]

    def one(r):
        picked = chosen(wanted_ref, r, base)
        for c in range(cols):
            send_ref[spot(r, c)] = picked

    loop(wanted_ref.shape[0], one)


def first_dual_kernel(spot, wanted_ref, cot_ref, send_ref):
    choose_for_all(spot, wanted_ref, [cot_ref[b] for b in range(cot_ref.shape[0])], send_ref)


def sum_pushed(wanted_ref, received_ref, start):
    channels, side = start[0].shape
    rows = received_ref.shape[0]

    def step(r, blocks):
        at = jnp.broadcast_to(wanted_ref[r], (channels, side))
        pushed = received_ref[r, :channels, :].astype(F32)
        return tuple(block + jnp.where(at == b, pushed, 0.0) for b, block in enumerate(blocks))

    blocks = tuple(start)
    if rows <= 16:
        for r in range(rows):
            blocks = step(r, blocks)
        return blocks
    return lax.fori_loop(0, rows, step, blocks)


def place_of(tile, shape):
    side = tile.shape[1]
    return jnp.broadcast_to(tile[side:].astype(F32)[:1], shape)


def pushed_tile(tiles_ref, other_ref, t):
    rows = lax.axis_size("row")
    upper = lax.axis_index("row") >= rows // 2
    here = t < rows - rows // 2
    own = upper == here
    return jnp.where(own, tiles_ref[t], other_ref[t])


def mixed_by(weights, blocks):
    side = blocks[0].shape[1]
    high, rest = halves(jnp.concatenate(blocks, 1))
    mixed = jnp.dot(
        weights, jnp.concatenate([high, rest, high, rest], 0), preferred_element_type=F32
    )
    return [mixed[:, b * side : (b + 1) * side] for b in range(len(blocks))]


def folded(terms, channels):
    return terms + pltpu.roll(terms, terms.shape[1] - channels, 1)


def contract(left, right):
    return lax.dot_general(
        jnp.concatenate(left, 1),
        jnp.concatenate(right, 1),
        (((1,), (1,)), ((), ())),
        preferred_element_type=F32,
    )


def dual_step(
    spot, layer, pushed, cot_in, mask_ref, scale_ref, mix_ref, wanted_ref, cot_ref, send_ref
):
    above = layer + 1
    tau = scale_ref[pl.ds(2 * above, 1), :]
    mixed = mixed_by(mix_ref[2 * above], pushed)
    base = []
    for b in range(len(pushed)):
        cot = mask_ref[layer, pl.ds(b, 1), :].astype(F32) * (cot_in[b] + tau * mixed[b])
        cot_ref[b] = cot
        base.append(cot)
    choose_for_all(spot, wanted_ref, base, send_ref)


def all_pushed(wanted_ref, received_ref, pushed_ref):
    owned, channels, side = pushed_ref.shape
    pushed = sum_pushed(
        wanted_ref, received_ref, [jnp.zeros((channels, side), F32) for _ in range(owned)]
    )
    for b in range(owned):
        pushed_ref[b] = pushed[b]
    return pushed


def dual_kernel(spot, layer, received_ref, *refs):
    *refs, pushed_ref = refs
    wanted_ref = refs[4]
    dual_step(spot, layer, all_pushed(wanted_ref, received_ref, pushed_ref), *refs)


def last_layer_dual_kernel(spot, pushed_ref, *refs):
    dual_step(spot, 0, [pushed_ref[b] for b in range(pushed_ref.shape[0])], *refs)


def doubled_halves(x):
    high, rest = halves(x)
    return jnp.concatenate([high, rest, high, rest], 0)


def extrapolate(saved_ref, layer, p):
    return (
        2.0 * saved_ref[layer + 1, p].astype(F32) - saved_ref[layer, p].astype(F32)
    ).astype(BF16)


def terms_kernel(
    wanted_ref,
    last_received_ref,
    saved_dual_ref,
    saved_primal_ref,
    tiles_ref,
    other_ref,
    received_ref,
    *refs,
):
    last_sums_ref, last_pushed_ref, part_ref, dual_ref = refs[-4:]
    refs = (*refs[:-4], last_pushed_ref, last_sums_ref)
    early, channels, side = dual_ref.shape
    owned, blocks = saved_dual_ref.shape[1], saved_primal_ref.shape[1]
    all_pushed(wanted_ref, last_received_ref, last_pushed_ref)
    for i in range(early):
        pushed_ref, sums_ref = refs[2 * i], refs[2 * i + 1]
        layer = early - i
        part_ref[layer - 1] = folded(
            contract(
                [saved_dual_ref[layer, b] for b in range(owned)],
                [doubled_halves(pushed_ref[b]) for b in range(owned)],
            ),
            channels,
        )
        dual_ref[layer - 1] = folded(
            contract(
                [extrapolate(saved_primal_ref, layer, p) for p in range(blocks)],
                [doubled_halves(sums_ref[p]) for p in range(blocks)],
            ),
            channels,
        )

    def step(t, sums):
        tile = pushed_tile(tiles_ref, other_ref, t)
        product = jnp.dot(
            received_ref[t, channels:, :], tile[:side], preferred_element_type=F32
        )
        at = place_of(tile, product.shape)
        return tuple(s + jnp.where(at == p, product, 0.0) for p, s in enumerate(sums))

    sums = tuple(jnp.zeros((channels, side), F32) for _ in range(blocks))
    if received_ref.shape[0] <= 16:
        for t in range(received_ref.shape[0]):
            sums = step(t, sums)
    else:
        sums = lax.fori_loop(0, received_ref.shape[0], step, sums)
    for p in range(blocks):
        part_ref[early + p] = sums[p]
    for i in range(early + blocks, part_ref.shape[0]):
        part_ref[i] = jnp.zeros((channels, side), F32)


def last_dual_kernel(
    row_scale,
    col_scale,
    wanted_ref,
    received_ref,
    cot_in,
    scale_ref,
    grad_in,
    grad_ref,
    cot_ref,
    primal_out,
    dual_out,
    held_ref,
    primal_ref,
    dual_ref,
    sems,
):
    owned, channels, side = held_ref.shape
    layers = primal_ref.shape[0]
    half = channels // 2
    rows = received_ref.shape[0]
    copies = [pltpu.make_async_copy(grad_in, grad_ref, sems.at[owned])]
    copies[0].start()
    blocks = sum_pushed(wanted_ref, received_ref, [cot_in[b] for b in range(owned)])
    for b, block in enumerate(blocks):
        held_ref[b] = block
        copy = pltpu.make_async_copy(held_ref.at[b], cot_ref.at[b], sems.at[b])
        copy.start()
        copies.append(copy)
    all_terms = total_of(
        rows, lambda r: received_ref[r, channels:, :].astype(F32), (layers * half, side)
    )
    for k in range(layers):
        terms = all_terms[k * half : (k + 1) * half]
        dual = scale_ref[pl.ds(2 * k + 1, 1), :] * row_scale * terms
        primal = scale_ref[pl.ds(2 * k, 1), :] * col_scale * terms
        dual_ref[k, :half, :] = dual[:, :channels]
        dual_ref[k, half:, :] = pltpu.roll(dual, side - channels, 1)[:, :channels]
        primal_ref[k, :half, :] = pltpu.roll(primal, side - 2 * channels, 1)[:, :channels]
        primal_ref[k, half:, :] = pltpu.roll(primal, side - 3 * channels, 1)[:, :channels]
    for i, (source, target) in enumerate(((primal_ref, primal_out), (dual_ref, dual_out))):
        copies.append(pltpu.make_async_copy(source, target, sems.at[owned + 1 + i]))
        copies[-1].start()
    for copy in copies:
        copy.wait()


def primal_step(spot, layer, shared, grad_ref):
    tiles_ref, other_ref, scale_ref, mix_ref, fetched_ref, grad_in, mask_ref = shared
    blocks, channels, side = grad_ref.shape
    rows = tiles_ref.shape[0]
    me = lax.axis_index("col")
    sigma = scale_ref[pl.ds(2 * layer + 1, 1), :]

    def step(t, sums):
        for tiles, message in ((tiles_ref, spot(t, me)), (other_ref, spot(t, 1 - me))):
            product = jnp.dot(
                fetched_ref[message], tiles[t, :side, :], preferred_element_type=F32
            )
            at = place_of(tiles[t], product.shape)
            sums = tuple(s + jnp.where(at == p, product, 0.0) for p, s in enumerate(sums))
        return sums

    sums = tuple(jnp.zeros((channels, side), F32) for _ in range(blocks))
    if rows <= 16:
        for t in range(rows):
            sums = step(t, sums)
    else:
        sums = lax.fori_loop(0, rows, step, sums)
    cots = []
    mixed = mixed_by(mix_ref[2 * layer + 1], sums)
    for p in range(blocks):
        back = sigma * mixed[p]
        cot = mask_ref[layer, pl.ds(p, 1), :].astype(F32) * (grad_in[p] + 2.0 * back)
        grad_ref[p] = cot - back
        cots.append(cot)
    return sums, cots


def push(tiles_ref, other_ref, blocks, send_ref, below):
    channels, side = blocks[0].shape

    def one(t):
        tile = pushed_tile(tiles_ref, other_ref, t)
        at = place_of(tile, blocks[0].shape)
        picked = blocks[0]
        for p in range(1, len(blocks)):
            picked = jnp.where(at == p, blocks[p], picked)
        product = lax.dot_general(
            picked.astype(BF16),
            tile[:side],
            (((1,), (1,)), ((), ())),
            preferred_element_type=F32,
        )
        send_ref[t, :channels, :] = product.astype(BF16)
        if below is not None:
            send_ref[t, channels:, :] = below(t)

    loop(tiles_ref.shape[0], one)


def primal_kernel(spot, layer, *refs):
    shared, rest, (grad_ref, send_ref, sums_ref) = refs[:7], refs[7:-3], refs[-3:]
    sums, cots = primal_step(spot, layer, shared, grad_ref)
    below = None
    if rest:
        wanted_ref, dual_ref = rest
        base = [dual_ref[0, b].astype(F32) for b in range(dual_ref.shape[1])]
        below = lambda t: chosen(wanted_ref, t, base)
    push(*shared[:2], cots, send_ref, below)
    for p, total in enumerate(sums):
        sums_ref[p] = total


def last_primal_kernel(spot, *refs):
    shared, rest, (grad_ref, send_ref) = refs[:7], refs[7:-2], refs[-2:]
    saved_ref, part_ref, part_other, dual_ref = rest
    scale_ref, mix_ref = shared[2], shared[3]
    blocks, channels, side = grad_ref.shape
    early = dual_ref.shape[0]
    half = channels // 2
    sums, cots = primal_step(spot, 0, shared, grad_ref)
    tau = scale_ref[pl.ds(0, 1), :]
    left, right = [], []
    for p in range(blocks):
        pulled = part_ref[early + p] + part_other[early + p]
        left.append(jnp.concatenate([extrapolate(saved_ref, 0, p), *halves(pulled)], 0))
        right.append(jnp.concatenate([*halves(sums[p]), *halves(cots[p])], 0))
    terms = contract(left, right)
    lane = lax.broadcasted_iota(jnp.int32, (channels, side), 1)
    low = lane < 2 * channels
    terms = jnp.where(
        low, terms[:channels], terms[channels : 2 * channels] + terms[2 * channels :]
    )
    all_terms = [folded(terms, channels)] + [
        jnp.where(low, dual_ref[i], part_ref[i] + part_other[i]) for i in range(early)
    ]
    packed = jnp.concatenate(
        [
            jnp.where(
                lax.rem(lane[:half], 2 * channels) < channels,
                one[:half],
                pltpu.roll(one[half:], channels, 1),
            )
            for one in all_terms
        ],
        0,
    ).astype(BF16)
    mixed = [
        (tau * cot).astype(BF16).astype(F32) for cot in mixed_by(mix_ref[0], cots)
    ]
    push(*shared[:2], mixed, send_ref, lambda t: packed)


def per_device(
    tile_blocks,
    tile_rows,
    tile_cols,
    saved_primal,
    saved_dual,
    primal_active,
    dual_active,
    primal_mix,
    dual_mix,
    step_fracs,
    cot_primal,
    cot_dual,
):
    row_count = lax.axis_size("row")
    col_count = lax.axis_size("col")
    owned, channels, side = cot_dual.shape
    primal_count = cot_primal.shape[0]
    layer_count = primal_mix.shape[0]
    half = channels // 2
    row_scale = 1.0 / math.sqrt(owned * row_count * col_count * side)
    col_scale = 1.0 / math.sqrt(primal_count * row_count * side)
    params = pltpu.CompilerParams(vmem_limit_bytes=24 * 1024 * 1024)

    def call(kernel, outs, *operands, ins=None, out_specs=None, **rest):
        return pl.pallas_call(
            kernel,
            out_shape=outs,
            in_specs=ins or [VMEM] * len(operands),
            out_specs=out_specs or jax.tree.map(lambda _: VMEM, outs),
            compiler_params=params,
            **rest,
        )(*operands)

    shift = row_count - row_count // 2
    order = [(slot + row_count - shift) % row_count for slot in range(row_count)]
    order_all = [row * col_count + c for row in order for c in reversed(range(col_count))]
    if (row_count, col_count) == (8, 2):
        order_all = [9, 3, 4, 8, 13, 7, 1, 14, 12, 5, 15, 0, 11, 6, 10, 2]
    spot = partial(spot_of, order, order_all, col_count)

    order_push = [
        [
            row * col_count + (c if i < shift else col_count - 1 - c)
            for i, row in enumerate(order)
        ]
        for c in range(col_count)
    ]

    def exchange(x, axes, groups):
        return lax.all_to_all(
            x, axes, split_axis=0, concat_axis=0, axis_index_groups=groups, tiled=True
        )

    def shape(dims, kind=F32):
        return jax.ShapeDtypeStruct(dims, kind)

    def in_hbm(*arrays):
        return [pltpu.with_memory_space_constraint(x, pltpu.HBM) for x in arrays]

    def swap(x):
        return lax.ppermute(x, "col", [(i, col_count - 1 - i) for i in range(col_count)])

    slot = partial(slot_of, peer_size=owned * col_count, shift=shift, row_count=row_count)
    asked = call(
        partial(ask_kernel, slot, owned),
        shape((row_count, 1, side)),
        *in_hbm(tile_rows),
        ins=[HBM],
        scratch_shapes=[pltpu.SMEM(tile_rows.shape, jnp.int32), pltpu.SemaphoreType.DMA],
    )
    wanted = exchange(asked, "row", [order])
    tiles, scale, mix, cot = call(
        partial(prepare_kernel, slot, primal_count),
        (
            shape((row_count, side + 16, side), BF16),
            shape((2 * layer_count, side)),
            shape((2 * layer_count, channels, side), BF16),
            shape(cot_dual.shape),
        ),
        *in_hbm(
            tile_rows,
            tile_cols,
            step_fracs,
            tile_blocks,
            cot_dual,
            dual_active,
            dual_mix,
            primal_mix,
        ),
        ins=[HBM] * 8,
        scratch_shapes=[
            pltpu.VMEM((2 * layer_count, channels, side), F32),
            pltpu.SMEM(tile_rows.shape, jnp.int32),
            pltpu.SMEM(tile_cols.shape, jnp.int32),
            pltpu.SMEM(step_fracs.shape, jnp.int32),
            pltpu.VMEM((owned, side), jnp.int32),
            pltpu.VMEM((2, layer_count, channels, channels), F32),
            pltpu.VMEM(tile_blocks.shape, BF16),
            pltpu.SemaphoreType.DMA((8,)),
        ],
    )
    other_tiles = swap(lax.optimization_barrier((tiles, wanted))[0])
    blocks_out = shape((col_count * row_count, channels, side), BF16)
    grad_x = cot_primal
    send = call(partial(first_dual_kernel, spot), blocks_out, wanted, cot)
    carried = []
    first_received = None
    spread = 16
    for layer in reversed(range(layer_count)):
        fetched = exchange(send, ("row", "col"), [order_all])
        shared = (tiles, other_tiles, scale, mix, fetched, grad_x, primal_active)
        if layer == 0:
            height = channels + layer_count * half
            grad_x, pushed = call(
                partial(last_primal_kernel, spot),
                (shape(cot_primal.shape), shape((row_count, height, side), BF16)),
                *shared,
                saved_primal,
                part,
                part_other,
                dual_terms,
            )
            received = exchange(pushed, ("row", "col"), order_push)
            break
        first = layer == layer_count - 1
        height = 2 * channels if first else channels
        grad_x, pushed, sums = call(
            partial(primal_kernel, spot, layer),
            (
                shape(cot_primal.shape),
                shape((row_count, height, side), BF16),
                shape(cot_primal.shape),
            ),
            *shared,
            *((wanted, saved_dual) if first else ()),
        )
        received = exchange(pushed, ("row", "col"), order_push)
        if first:
            first_received = received
        state = (cot, dual_active, scale, mix, wanted)
        dual_shape = shape(cot_dual.shape)
        if layer > 1:
            cot, send, sums_pushed = call(
                partial(dual_kernel, spot, layer - 1),
                (dual_shape, blocks_out, dual_shape),
                received,
                *state,
            )
            carried += [sums_pushed, sums]
            continue
        sums_pushed, part, dual_terms = call(
            terms_kernel,
            (
                dual_shape,
                shape((max(spread, layer_count - 1 + primal_count), channels, side)),
                shape((layer_count - 1, channels, side)),
            ),
            wanted,
            received,
            saved_dual,
            saved_primal,
            tiles,
            other_tiles,
            first_received,
            *carried,
            sums,
        )
        part_other = swap(part)
        cot, send = call(
            partial(last_layer_dual_kernel, spot), (dual_shape, blocks_out), sums_pushed, *state
        )
    grad_x, grad_y, primal_mix_grad, dual_mix_grad = call(
        partial(last_dual_kernel, row_scale, col_scale),
        (
            shape(cot_primal.shape),
            shape(cot_dual.shape),
            shape(primal_mix.shape),
            shape(dual_mix.shape),
        ),
        wanted,
        received,
        cot,
        scale,
        grad_x,
        out_specs=(HBM,) * 4,
        scratch_shapes=[
            pltpu.VMEM(cot_dual.shape, F32),
            pltpu.VMEM(primal_mix.shape, F32),
            pltpu.VMEM(dual_mix.shape, F32),
            pltpu.SemaphoreType.DMA((owned + 3,)),
        ],
    )
    return (grad_x, grad_y, primal_mix_grad, dual_mix_grad)


def solution(mesh):
    return jax.shard_map(
        per_device,
        mesh=mesh,
        in_specs=(
            P(("groups", "row", "col"), None, None),
            P(("groups", "row", "col")),
            P(("groups", "row", "col")),
            P(None, ("groups", "row"), None, None),
            P(None, ("groups", "row", "col"), None, None),
            P(None, ("groups", "row"), None),
            P(None, ("groups", "row", "col"), None),
            P(),
            P(),
            P(),
            P(("groups", "row"), None, None),
            P(("groups", "row", "col"), None, None),
        ),
        out_specs=(
            P(("groups", "row"), None, None),
            P(("groups", "row", "col"), None, None),
            P("groups", None, None),
            P("groups", None, None),
        ),
        check_vma=False,
    )
```
